32 devices in a mesh: ty: 8 (over y, x, core), tx: 4 (over z).
Axes of the slice: x: 2, y: 2, z: 4, core: 2. Of those that a mesh axis runs over, the one named last changes fastest.
Arguments:
- object_slices: float32 [2, 2, 1024, 512], P(None, None, 'ty', 'tx'), may hold values from -5 to 5
- probe: float32 [4, 2, 128, 128], replicated, may hold values from -4 to 4
- measured: float32 [8, 4, 4, 128, 128], P('ty', 'tx'), may hold values from 0 to 2
- offsets: int32 [2, 8, 4, 4], P(None, 'ty', 'tx'), may hold values from 0 to 127, as said below
- counts: int32 [8, 4], P('ty', 'tx'), may hold values from 1 to 4, as said below
Outputs:
- object_grad: float32 [2, 2, 1024, 512], P(None, None, 'ty', 'tx')
- probe_grad: float32 [4, 2, 128, 128], replicated
The draws below stay inside these ranges and needn't reach their ends.
Inputs may be any that keep to these rules, and one draw needn't show every extreme that they name: `counts`: each tile has 1 to 4 live slots, and some tile has all 4 live. Every window lies inside the object: in the last tile row (column) the row (column) offset is at most 0. Slot 0 of every tile sits at the largest row and column offsets that its tile allows.
All inputs are finite; a program needn't handle non-finite values.
Results may differ from the reference program's by a relative error of at most 0.0003.
Values sent between devices are 32-bit elements; how exact they have to be, the bound alone decides.
No kernel may reach another device: no remote copies, remote signals or barrier semaphores. Data moves between devices by JAX's collectives and lax.ppermute only.
A program may use at most 64 MiB of HBM per device.

```python
import math
import jax
import jax.numpy as jnp
from jax import lax

WINDOW = 128
MODES = 4
SLICES = 2
TILE = 128
CAP = 4
TILES_Y = 8
TILES_X = 4
NY = 1024
NX = 512


def draw_counts(key, part):
    base_key, pick_key = jax.random.split(jax.random.fold_in(key, 11))
    total = TILES_Y * TILES_X
    base = jax.random.randint(base_key, (total,), 1, CAP + 1)
    chosen = jax.random.randint(pick_key, (), 0, total)
    filled = jnp.where(jnp.arange(total) == chosen, CAP, base)
    return filled.reshape(TILES_Y, TILES_X).astype(jnp.int32)


def draw_offsets(key, part):
    row_key, col_key = jax.random.split(jax.random.fold_in(key, 23))
    row_ids = jnp.arange(TILES_Y)[:, None, None]
    col_ids = jnp.arange(TILES_X)[None, :, None]
    row_high = jnp.where(row_ids == TILES_Y - 1, TILE - WINDOW, TILE - 1) + jnp.zeros((TILES_Y, TILES_X, CAP), jnp.int32)
    col_high = jnp.where(col_ids == TILES_X - 1, TILE - WINDOW, TILE - 1) + jnp.zeros((TILES_Y, TILES_X, CAP), jnp.int32)
    rows = jax.random.randint(row_key, (TILES_Y, TILES_X, CAP), 0, row_high + 1)
    cols = jax.random.randint(col_key, (TILES_Y, TILES_X, CAP), 0, col_high + 1)
    first = jnp.arange(CAP)[None, None, :] == 0
    rows = jnp.where(first, row_high, rows)
    cols = jnp.where(first, col_high, cols)
    return jnp.stack([rows, cols]).astype(jnp.int32)


def block_scale(own_key, dims, cuts, smallest, top_value):
    factor_of = 1.0
    for dim, shards_of in cuts:
        draws = jax.random.uniform(jax.random.fold_in(jax.random.fold_in(own_key, 6), dim), (shards_of,), jnp.float32, smallest / len(cuts), top_value / len(cuts))
        factor_of = factor_of * jnp.repeat(jnp.exp(draws), dims[dim] // shards_of).reshape((-1,) + (1,) * (len(dims) - 1 - dim))
    return factor_of


def gaussian(key, shape, deviation, limit, pieces=(), kind=jnp.bfloat16):
    entries = deviation * jax.random.normal(key, shape, jnp.float32)
    if pieces:
        entries = entries * block_scale(key, shape, pieces, -0.22, 0.18)
    return jnp.clip(entries, -limit, limit).astype(kind)


def setup_inputs(seed: int = 0) -> dict:
    arg_keys = jax.random.split(jax.random.key(seed), 6)
    object_slices = gaussian(arg_keys[0], (SLICES, 2, NY, NX), 0.7, 5.0, ((2, 8), (3, 4)), jnp.float32)
    probe = gaussian(arg_keys[1], (MODES, 2, WINDOW, WINDOW), 0.5, 4.0, (), jnp.float32)
    measured = jnp.clip(2.0 * jax.random.uniform(arg_keys[2], (TILES_Y, TILES_X, CAP, WINDOW, WINDOW), jnp.float32) ** block_scale(arg_keys[2], (TILES_Y, TILES_X, CAP, WINDOW, WINDOW), ((0, 8), (1, 4)), -0.2, 0.2), 0.0, 2.0)
    offsets = draw_offsets(jax.random.fold_in(arg_keys[5], 71), 0)
    counts = draw_counts(jax.random.fold_in(arg_keys[5], 71), 0)
    return dict(object_slices=object_slices, probe=probe, measured=measured, offsets=offsets, counts=counts)


def propagator_table():
    positions = jnp.arange(WINDOW, dtype=jnp.int32)
    freq = (positions + WINDOW // 2) % WINDOW - WINDOW // 2
    quad = (freq[:, None] * freq[:, None] + freq[None, :] * freq[None, :]) % (4 * WINDOW)
    angle = quad.astype(jnp.float32) * (-2.0 * math.pi / (4 * WINDOW))
    return lax.complex(jnp.cos(angle), jnp.sin(angle))

def tile_loss(windows, probe, measured_tile, live):
    propagator = propagator_table()
    probe_c = lax.complex(probe[:, 0], probe[:, 1])
    window_c = lax.complex(windows[:, :, 0], windows[:, :, 1])
    wave = probe_c[None] * window_c[:, 0][:, None]
    for layer in range(1, SLICES):
        spectrum = jnp.fft.fft2(wave, norm='ortho') * propagator
        wave = jnp.fft.ifft2(spectrum, norm='ortho') * window_c[:, layer][:, None]
    far_field = jnp.fft.fft2(wave, norm='ortho')
    intensity = lax.optimization_barrier(jnp.sum(jnp.real(far_field) ** 2 + jnp.imag(far_field) ** 2, axis=1))
    diff = (intensity - measured_tile) * live[:, None, None]
    return 0.5 * jnp.sum(diff * diff)

def reference(object_slices, probe, measured, offsets, counts):
    zero = jnp.zeros((), jnp.int32)

    def one_tile(carry, tile_id):
        grad_object, grad_probe = carry
        tile_row = (tile_id // TILES_X).astype(jnp.int32)
        tile_col = (tile_id % TILES_X).astype(jnp.int32)
        local = lax.dynamic_slice(offsets, (zero, tile_row, tile_col, zero), (2, 1, 1, CAP)).reshape(2, CAP)
        rows_at = (tile_row * TILE + local[0]).astype(jnp.int32)
        cols_at = (tile_col * TILE + local[1]).astype(jnp.int32)

        def cut_window(row_at, col_at):
            return lax.dynamic_slice(object_slices, (zero, zero, row_at, col_at), (SLICES, 2, WINDOW, WINDOW))
        windows = jax.vmap(cut_window)(rows_at, cols_at)
        measured_tile = lax.dynamic_slice(measured, (tile_row, tile_col, zero, zero, zero), (1, 1, CAP, WINDOW, WINDOW)).reshape(CAP, WINDOW, WINDOW)
        count = lax.dynamic_slice(counts, (tile_row, tile_col), (1, 1)).reshape(())
        live = (jnp.arange(CAP, dtype=jnp.int32) < count).astype(jnp.float32)
        loss_value, pull = jax.vjp(lambda wins, prb: tile_loss(wins, prb, measured_tile, live), windows, probe)
        grad_windows, grad_probe_tile = pull(jnp.ones_like(loss_value))

        def add_slot(slot, total):
            start = (zero, zero, rows_at[slot], cols_at[slot])
            current = lax.dynamic_slice(total, start, (SLICES, 2, WINDOW, WINDOW))
            return lax.dynamic_update_slice(total, current + grad_windows[slot], start)
        grad_object = lax.fori_loop(0, CAP, add_slot, grad_object)
        return ((grad_object, grad_probe + grad_probe_tile), None)
    start_carry = (jnp.zeros_like(object_slices), jnp.zeros_like(probe))
    (object_grad, probe_grad), _ = lax.scan(one_tile, start_carry, jnp.arange(TILES_Y * TILES_X, dtype=jnp.int32))
    return (object_grad, probe_grad)
```

```python
import functools

import jax
import jax.numpy as jnp
import numpy as np
from jax import lax
from jax.experimental import pallas as pl
from jax.experimental.pallas import tpu as pltpu
from jax.sharding import PartitionSpec as P

BF16 = jnp.bfloat16
F32 = jnp.float32


def moved(array, axis, by):
    length = lax.axis_size(axis)
    pairs = [(i, i + by) for i in range(length) if 0 <= i + by < length]
    return lax.ppermute(array, axis, pairs)


def moved_both(array, rows_by, cols_by):
    rows, cols = lax.axis_size("ty"), lax.axis_size("tx")
    pairs = [
        (a * cols + b, (a + rows_by) * cols + b + cols_by)
        for a in range(rows)
        for b in range(cols)
        if 0 <= a + rows_by < rows and 0 <= b + cols_by < cols
    ]
    return lax.ppermute(array, ("ty", "tx"), pairs)


def swapped(array, axis, bit):
    length = lax.axis_size(axis)
    return lax.ppermute(array, axis, [(i, i ^ bit) for i in range(length)])


def summed_everywhere(array):
    shape = array.shape
    steps = []
    for axis in ("ty", "tx"):
        bit = 1
        while bit < lax.axis_size(axis):
            steps.append((axis, bit))
            bit *= 2
    part = array.reshape(-1, shape[-1])
    for axis, bit in steps:
        half = part.shape[0] // 2
        side = (lax.axis_index(axis) // bit) % 2
        mine = lax.dynamic_slice_in_dim(part, side * half, half, 0)
        other = lax.dynamic_slice_in_dim(part, (1 - side) * half, half, 0)
        part = mine + swapped(other, axis, bit)
    for axis, bit in steps[::-1]:
        side = (lax.axis_index(axis) // bit) % 2
        other = swapped(part, axis, bit)
        low = jnp.where(side == 0, part, other)
        high = jnp.where(side == 0, other, part)
        part = jnp.concatenate([low, high], axis=0)
    return part.reshape(shape)


def real_forms(table):
    right = np.block([[table.real, table.imag], [-table.imag, table.real]]).astype(np.float32)
    high = right.astype(BF16)
    low = (right - high.astype(np.float32)).astype(BF16)
    return (
        np.concatenate([high, high, low], axis=0),
        np.concatenate([high.T, high.T, low.T], axis=1),
    )


def tables(size):
    positions = np.arange(size)
    dft = np.exp(-2j * np.pi * (positions[:, None] * positions[None, :] % size) / size) / np.sqrt(size)
    freq = (positions + size // 2) % size - size // 2
    chirp = np.exp(-2j * np.pi * (freq * freq % (4 * size)) / (4 * size))
    through = dft.conj() @ (chirp[:, None] * dft)
    return real_forms(dft), real_forms(through)


def halves(x):
    high = x.astype(BF16)
    return high, (x - high.astype(F32)).astype(BF16)


def from_right(x, table):
    high, low = halves(x)
    return jnp.dot(jnp.concatenate([high, low, high], axis=1), table, preferred_element_type=F32)


def from_left(x, table):
    high, low = halves(x)
    return jnp.dot(table, jnp.concatenate([high, low, high], axis=0), preferred_element_type=F32)


def rows_to_lanes(x, size):
    count = x.shape[0] // size
    parts = [x[m * size:(m + 1) * size] for m in range(count)]
    return jnp.concatenate(
        [jnp.concatenate([p[:, :size] for p in parts], axis=1),
         jnp.concatenate([p[:, size:] for p in parts], axis=1)], axis=0)


def both_sides(fields, right_table, left_table):
    size = fields[0][0].shape[-1]
    x = jnp.concatenate([jnp.concatenate([re, im], axis=1) for re, im in fields], axis=0)
    y = rows_to_lanes(from_right(x, right_table), size)
    z = from_left(y, left_table)
    return [
        (z[:size, m * size:(m + 1) * size], z[size:, m * size:(m + 1) * size])
        for m in range(len(fields))
    ]


def product(a, b):
    return (a[0] * b[0] - a[1] * b[1], a[0] * b[1] + a[1] * b[0])


def fill(wide, own, right, down, corner, size):
    wide[:, :size, :size] = own[...]
    wide[:, :size, size:] = right[...]
    wide[:, size:, :size] = down[...]
    wide[:, size:, size:] = corner[...]


SUBLANES = 8


def window_of(wide, at, slot, size):
    row, col = at[0, slot], at[1, slot]
    shift = lax.rem(row, SUBLANES)
    rows = pl.ds(pl.multiple_of(row - shift, SUBLANES), size + SUBLANES)
    left = lax.rem(2 * size - col, 2 * size)
    up = lax.rem(size + SUBLANES - shift, size + SUBLANES)
    return [
        pltpu.roll(pltpu.roll(wide[c, rows, :], left, axis=1)[:, :size], up, axis=0)[:size]
        for c in range(2)
    ]


def add_window(total, at, slot, grads, size):
    row, col = at[0, slot], at[1, slot]
    shift = lax.rem(row, SUBLANES)
    rows = pl.ds(pl.multiple_of(row - shift, SUBLANES), size + SUBLANES)
    for c in range(2):
        taller = jnp.concatenate([grads[c], jnp.zeros((SUBLANES, size), F32)], axis=0)
        lowered = pltpu.roll(taller, shift, axis=0)
        padded = jnp.concatenate([lowered, jnp.zeros_like(lowered)], axis=1)
        total[c, rows, :] += pltpu.roll(padded, col, axis=1)


def give(total, own, right, down, corner, size):
    own[...] = total[:, :size, :size]
    right[...] = total[:, :size, size:]
    down[...] = total[:, size:, :size]
    corner[...] = total[:, size:, size:]


def first_kernel(at, own, right, down, corner, probe, right_table, left_table, psi, window, wide):
    size = own.shape[-1]
    modes = probe.shape[0]
    slot = pl.program_id(0)

    @pl.when(slot == 0)
    def _():
        fill(wide, own, right, down, corner, size)

    w = window_of(wide, at, slot, size)
    window[0, 0], window[0, 1] = w[0], w[1]
    fields = [product((probe[m, 0], probe[m, 1]), w) for m in range(modes)]
    waves = both_sides(fields, right_table[...], left_table[...])
    for m in range(modes):
        psi[0, m, 0], psi[0, m, 1] = waves[m]


def second_kernel(at, count, own, right, down, corner, psi, measured, right_table, left_table,
                  back, g_own, g_right, g_down, g_corner, wide, total):
    size = own.shape[-1]
    modes = psi.shape[1]
    slot = pl.program_id(0)

    @pl.when(slot == 0)
    def _():
        fill(wide, own, right, down, corner, size)
        total[...] = jnp.zeros_like(total)

    w = window_of(wide, at, slot, size)
    fields = [product((psi[0, m, 0], psi[0, m, 1]), w) for m in range(modes)]
    far = both_sides(fields, right_table[...], left_table[...])
    intensity = sum(re * re + im * im for re, im in far)
    live = jnp.where(slot < count[0], 2.0, 0.0).astype(F32)
    diff = (intensity - measured[0]) * live
    conj = both_sides([(re * diff, -(im * diff)) for re, im in far], right_table[...], left_table[...])
    g_re, g_im = 0.0, 0.0
    for m in range(modes):
        back[0, m, 0], back[0, m, 1] = product(conj[m], w)
        re, im = product(conj[m], (psi[0, m, 0], psi[0, m, 1]))
        g_re, g_im = g_re + re, g_im - im
    add_window(total, at, slot, (g_re, g_im), size)

    @pl.when(slot == pl.num_programs(0) - 1)
    def _():
        give(total, g_own, g_right, g_down, g_corner, size)


def third_kernel(at, back, window, probe, right_table, left_table,
                 g_probe, g_own, g_right, g_down, g_corner, total):
    size = window.shape[-1]
    modes = probe.shape[0]
    slot = pl.program_id(0)

    @pl.when(slot == 0)
    def _():
        total[...] = jnp.zeros_like(total)
        g_probe[...] = jnp.zeros_like(g_probe)

    conj = both_sides(
        [(back[0, m, 0], back[0, m, 1]) for m in range(modes)], right_table[...], left_table[...]
    )
    w = (window[0, 0], window[0, 1])
    g_re, g_im = 0.0, 0.0
    for m in range(modes):
        re, im = product(conj[m], w)
        g_probe[m, 0] += re
        g_probe[m, 1] -= im
        re, im = product(conj[m], (probe[m, 0], probe[m, 1]))
        g_re, g_im = g_re + re, g_im - im
    add_window(total, at, slot, (g_re, g_im), size)

    @pl.when(slot == pl.num_programs(0) - 1)
    def _():
        give(total, g_own, g_right, g_down, g_corner, size)


def whole(shape):
    return pl.BlockSpec(shape, lambda s: (0,) * len(shape))


def by_slot(shape):
    return pl.BlockSpec((1,) + shape[1:], lambda s: (s,) + (0,) * (len(shape) - 1))


SCALARS = pl.BlockSpec(memory_space=pltpu.SMEM)


def call(kernel, slots, args, in_specs, outs, out_specs, scratch, flops):
    return pl.pallas_call(
        kernel,
        grid=(slots,),
        in_specs=in_specs,
        out_specs=out_specs,
        out_shape=[jax.ShapeDtypeStruct(s, F32) for s in outs],
        scratch_shapes=[pltpu.VMEM(s, F32) for s in scratch],
        compiler_params=pltpu.CompilerParams(vmem_limit_bytes=48 * 1024 * 1024),
        cost_estimate=pl.CostEstimate(flops=flops, bytes_accessed=4 * 1024 * 1024, transcendentals=0),
    )(*args)


def halo(tile):
    return tile, moved(tile, "tx", -1), moved(tile, "ty", -1), moved_both(tile, -1, -1)


def returned(own, right, down, corner):
    return (own + moved(right, "tx", 1)) + (moved(down, "ty", 1) + moved_both(corner, 1, 1))


def on_device(object_slices, probe, measured, offsets, counts):
    size = object_slices.shape[-1]
    slots = offsets.shape[-1]
    modes = probe.shape[0]
    at = offsets.reshape(2, slots)
    count = counts.reshape(1)
    (dft_right, dft_left), (through_right, through_left) = tables(size)
    tile = (2, size, size)
    wide = (2, 2 * size, 2 * size)
    field = (slots, modes, 2, size, size)
    right_t, left_t = dft_right.shape, dft_left.shape
    flops = slots * modes * 2 * size * (2 * size) * (6 * size) * 2

    psi, window = call(
        first_kernel, slots,
        (at, *halo(object_slices[0]), probe, through_right, through_left),
        [SCALARS] + [whole(tile)] * 4 + [whole(probe.shape), whole(right_t), whole(left_t)],
        [field, (slots, 2, size, size)],
        [by_slot(field), by_slot((slots, 2, size, size))],
        [wide], flops,
    )
    back, *grad_1 = call(
        second_kernel, slots,
        (at, count, *halo(object_slices[1]), psi, measured.reshape(slots, size, size), dft_right, dft_left),
        [SCALARS, SCALARS] + [whole(tile)] * 4
        + [by_slot(field), by_slot((slots, size, size)), whole(right_t), whole(left_t)],
        [field] + [tile] * 4,
        [by_slot(field)] + [whole(tile)] * 4,
        [wide, wide], 2 * flops,
    )
    grad_probe, *grad_0 = call(
        third_kernel, slots,
        (at, back, window, probe, through_right, through_left),
        [SCALARS, by_slot(field), by_slot((slots, 2, size, size)), whole(probe.shape), whole(right_t), whole(left_t)],
        [probe.shape] + [tile] * 4,
        [whole(probe.shape)] + [whole(tile)] * 4,
        [wide], flops,
    )
    object_grad = jnp.stack([returned(*grad_0), returned(*grad_1)])
    return object_grad, summed_everywhere(grad_probe)


def solution(mesh):
    in_specs = (
        P(None, None, "ty", "tx"),
        P(),
        P("ty", "tx", None, None, None),
        P(None, "ty", "tx", None),
        P("ty", "tx"),
    )
    out_specs = (P(None, None, "ty", "tx"), P())
    return jax.shard_map(
        on_device, mesh=mesh, in_specs=in_specs, out_specs=out_specs, check_vma=False
    )
```

```python
import functools

import jax
import jax.numpy as jnp
import numpy as np
from jax import lax
from jax.experimental import pallas as pl
from jax.experimental.pallas import tpu as pltpu
from jax.sharding import PartitionSpec as P

BF16 = jnp.bfloat16
F32 = jnp.float32


def moved(array, axis, by):
    length = lax.axis_size(axis)
    pairs = [(i, i + by) for i in range(length) if 0 <= i + by < length]
    return lax.ppermute(array, axis, pairs)


def moved_both(array, rows_by, cols_by):
    rows, cols = lax.axis_size("ty"), lax.axis_size("tx")
    pairs = [
        (a * cols + b, (a + rows_by) * cols + b + cols_by)
        for a in range(rows)
        for b in range(cols)
        if 0 <= a + rows_by < rows and 0 <= b + cols_by < cols
    ]
    return lax.ppermute(array, ("ty", "tx"), pairs)


def swapped(array, axis, bit):
    length = lax.axis_size(axis)
    return lax.ppermute(array, axis, [(i, i ^ bit) for i in range(length)])


def picked(array, index):
    return lax.dynamic_index_in_dim(array, index, 0, keepdims=False)


def scattered(part, axis, unit, ways):
    me = (lax.axis_index(axis) // unit) % ways
    blocks = part.reshape(ways, -1, part.shape[-1])
    others = [swapped(picked(blocks, me ^ d), axis, d * unit) for d in range(1, ways)]
    return functools.reduce(jnp.add, others, picked(blocks, me))


def gathered(part, axis, unit, ways):
    me = (lax.axis_index(axis) // unit) % ways
    out = jnp.zeros((ways,) + part.shape, part.dtype)
    out = lax.dynamic_update_index_in_dim(out, part, me, 0)
    for d in range(1, ways):
        out = lax.dynamic_update_index_in_dim(out, swapped(part, axis, d * unit), me ^ d, 0)
    return out.reshape(-1, part.shape[-1])


def real_forms(table):
    right = np.block([[table.real, table.imag], [-table.imag, table.real]]).astype(np.float32)
    high = right.astype(BF16)
    low = (right - high.astype(np.float32)).astype(BF16)
    return (
        np.concatenate([high, high, low], axis=0),
        np.concatenate([high.T, high.T, low.T], axis=1),
    )


def tables(size):
    positions = np.arange(size)
    dft = np.exp(-2j * np.pi * (positions[:, None] * positions[None, :] % size) / size) / np.sqrt(size)
    freq = (positions + size // 2) % size - size // 2
    chirp = np.exp(-2j * np.pi * (freq * freq % (4 * size)) / (4 * size))
    through = dft.conj() @ (chirp[:, None] * dft)
    return real_forms(dft), real_forms(through)


def halves(x):
    high = x.astype(BF16)
    return high, (x - high.astype(F32)).astype(BF16)


def from_right(x, table):
    high, low = halves(x)
    return jnp.dot(jnp.concatenate([high, low, high], axis=1), table, preferred_element_type=F32)


def from_left(x, table):
    high, low = halves(x)
    return jnp.dot(table, jnp.concatenate([high, low, high], axis=0), preferred_element_type=F32)


def both_sides(fields, right_table, left_table):
    size = fields[0][0].shape[-1]
    done = []
    for first in range(0, len(fields), 2):
        pair = fields[first:first + 2]
        x = jnp.concatenate([jnp.concatenate(field, axis=1) for field in pair], axis=0)
        y = from_right(x, right_table)
        rows = [y[k * size:(k + 1) * size] for k in range(len(pair))]
        y = jnp.concatenate(
            [jnp.concatenate([r[:, :size], r[:, size:]], axis=0) for r in rows], axis=1
        )
        z = from_left(y, left_table)
        for k in range(len(pair)):
            lanes = slice(k * size, (k + 1) * size)
            done.append((z[:size, lanes], z[size:, lanes]))
    return done


def product(a, b):
    return (a[0] * b[0] - a[1] * b[1], a[0] * b[1] + a[1] * b[0])


def fill(wide, layer, own, right, down, corner, size):
    wide[:, :size, :size] = own[layer]
    wide[:, :size, size:] = right[...]
    wide[:, size:, :size] = down[layer]
    wide[:, size:, size:] = corner[...]


SUBLANES = 8


def window_of(wide, at, slot, size):
    row, col = at[0, slot], at[1, slot]
    shift = lax.rem(row, SUBLANES)
    rows = pl.ds(pl.multiple_of(row - shift, SUBLANES), size + SUBLANES)
    left = lax.rem(2 * size - col, 2 * size)
    up = lax.rem(size + SUBLANES - shift, size + SUBLANES)
    return [
        pltpu.roll(pltpu.roll(wide[c, rows, :], left, axis=1)[:, :size], up, axis=0)[:size]
        for c in range(2)
    ]


def add_window(total, at, slot, grads, size):
    row, col = at[0, slot], at[1, slot]
    shift = lax.rem(row, SUBLANES)
    rows = pl.ds(pl.multiple_of(row - shift, SUBLANES), size + SUBLANES)
    for c in range(2):
        taller = jnp.concatenate([grads[c], jnp.zeros((SUBLANES, size), F32)], axis=0)
        lowered = pltpu.roll(taller, shift, axis=0)
        padded = jnp.concatenate([lowered, jnp.zeros_like(lowered)], axis=1)
        total[c, rows, :] += pltpu.roll(padded, col, axis=1)


def stage_kernel(*refs):
    count = (len(refs) - 1) // 2
    sources, targets, sems = refs[:count], refs[count:2 * count], refs[-1]
    copies = [pltpu.make_async_copy(a, b, sems.at[i]) for i, (a, b) in enumerate(zip(sources, targets))]
    for copy in copies:
        copy.start()
    for copy in copies:
        copy.wait()


def first_kernel(at, own, right, down, corner, probe, right_table, left_table, psi, window, wide):
    size = own.shape[-1]
    slots, modes = psi.shape[:2]
    fill(wide, 0, own, right, down, corner, size)
    fields = []
    for slot in range(slots):
        w = window_of(wide, at, slot, size)
        window[slot, 0], window[slot, 1] = w
        fields += [product((probe[m, 0], probe[m, 1]), w) for m in range(modes)]
    waves = both_sides(fields, right_table[...], left_table[...])
    for i, wave in enumerate(waves):
        psi[i // modes, i % modes, 0], psi[i // modes, i % modes, 1] = wave


def second_kernel(at, count, own, right, down, corner, psi, window, probe, measured,
                  dft_right, dft_left, through_right, through_left,
                  g_probe, g_upper, g_lower, wide, total):
    size = own.shape[-1]
    slots, modes = psi.shape[:2]
    fill(wide, 1, own, right, down, corner, size)
    total[...] = jnp.zeros_like(total)
    w = [window_of(wide, at, slot, size) for slot in range(slots)]
    waves = [[(psi[s, m, 0], psi[s, m, 1]) for m in range(modes)] for s in range(slots)]
    fields = [product(waves[s][m], w[s]) for s in range(slots) for m in range(modes)]
    far = both_sides(fields, dft_right[...], dft_left[...])
    fields = []
    for s in range(slots):
        own_far = far[s * modes:(s + 1) * modes]
        intensity = sum(re * re + im * im for re, im in own_far)
        live = jnp.where(s < count[0], 2.0, 0.0).astype(F32)
        diff = (intensity - measured[s]) * live
        fields += [(re * diff, -(im * diff)) for re, im in own_far]
    conj = both_sides(fields, dft_right[...], dft_left[...])
    fields = [product(conj[s * modes + m], w[s]) for s in range(slots) for m in range(modes)]
    start = both_sides(fields, through_right[...], through_left[...])
    for m in range(modes):
        parts = [product(start[s * modes + m], (window[s, 0], window[s, 1])) for s in range(slots)]
        g_probe[m, 0] = sum(re for re, _ in parts)
        g_probe[m, 1] = -sum(im for _, im in parts)
    for s in range(slots):
        for layer, (grads, by) in enumerate((
            (start, [(probe[m, 0], probe[m, 1]) for m in range(modes)]),
            (conj, waves[s]),
        )):
            parts = [product(grads[s * modes + m], by[m]) for m in range(modes)]
            pair = (sum(re for re, _ in parts), -sum(im for _, im in parts))
            add_window(total.at[layer], at, s, pair, size)
    g_upper[...] = total[:, :, :size, :]
    g_lower[...] = total[:, :, size:, :]


VMEM = pl.BlockSpec(memory_space=pltpu.VMEM)
SMEM = pl.BlockSpec(memory_space=pltpu.SMEM)
HBM = pl.BlockSpec(memory_space=pl.ANY)


def call(kernel, args, in_specs, outs, scratch, flops):
    return pl.pallas_call(
        kernel,
        in_specs=in_specs,
        out_specs=[VMEM] * len(outs),
        out_shape=[jax.ShapeDtypeStruct(shape, dtype) for shape, dtype in outs],
        scratch_shapes=scratch,
        compiler_params=pltpu.CompilerParams(vmem_limit_bytes=40 * 1024 * 1024),
        cost_estimate=pl.CostEstimate(flops=flops, bytes_accessed=4 * 1024 * 1024, transcendentals=0),
    )(*args)


def on_device(object_slices, probe, measured, offsets, counts):
    layers, _, _, size = object_slices.shape
    slots = offsets.shape[-1]
    modes = probe.shape[0]
    at = offsets.reshape(2, slots)
    count = counts.reshape(1)
    (dft_right, dft_left), (through_right, through_left) = tables(size)
    flops = slots * modes * 2 * size * (2 * size) * (6 * size) * 2
    wide = pltpu.VMEM((2, 2 * size, 2 * size), F32)

    rights = [moved(object_slices[k], "tx", -1) for k in range(layers)]
    corners = [moved_both(object_slices[k], -1, -1) for k in range(layers)]
    downs = moved(object_slices, "ty", -1)

    early = (probe, jnp.asarray(through_right), jnp.asarray(through_left))
    early = call(
        stage_kernel, early, [HBM] * 3, [(a.shape, a.dtype) for a in early],
        [pltpu.SemaphoreType.DMA((3,))], flops,
    )
    psi, window = call(
        first_kernel,
        (at, object_slices, rights[0], downs, corners[0], *early),
        [SMEM] + [VMEM] * 7,
        [((slots, modes, 2, size, size), F32), ((slots, 2, size, size), F32)],
        [wide], flops,
    )
    g_probe, g_upper, g_lower = call(
        second_kernel,
        (at, count, object_slices, rights[1], downs, corners[1], psi, window, early[0],
         measured.reshape(slots, size, size), dft_right, dft_left, early[1], early[2]),
        [SMEM] * 2 + [VMEM] * 12,
        [(probe.shape, F32)] + [((layers, 2, size, 2 * size), F32)] * 2,
        [wide, pltpu.VMEM((layers, 2, 2 * size, 2 * size), F32)], 3 * flops,
    )

    rows = lax.axis_size("ty")
    part = scattered(g_probe.reshape(-1, size), "ty", 1, 2)
    part = scattered(part, "ty", 2, rows // 2)
    part, g_lower = lax.optimization_barrier((part, g_lower))
    from_above = moved(g_lower, "ty", 1)
    bit = 1
    while bit < lax.axis_size("tx"):
        part = part + swapped(part, "tx", bit)
        bit *= 2
    g_wide = g_upper + from_above
    g_right, part = lax.optimization_barrier((g_wide[..., size:], part))
    from_left_tile = moved(g_right, "tx", 1)
    part = gathered(part, "ty", 2, rows // 2)
    part = gathered(part, "ty", 1, 2)
    object_grad = g_wide[..., :size] + from_left_tile
    return object_grad, part.reshape(probe.shape)


def solution(mesh):
    in_specs = (
        P(None, None, "ty", "tx"),
        P(),
        P("ty", "tx", None, None, None),
        P(None, "ty", "tx", None),
        P("ty", "tx"),
    )
    out_specs = (P(None, None, "ty", "tx"), P())
    return jax.shard_map(
        on_device, mesh=mesh, in_specs=in_specs, out_specs=out_specs, check_vma=False
    )
```

```python
import functools

import jax
import jax.numpy as jnp
import numpy as np
from jax import lax
from jax.experimental import pallas as pl
from jax.experimental.pallas import tpu as pltpu
from jax.sharding import PartitionSpec as P

BF16 = jnp.bfloat16
F32 = jnp.float32


def moved(array, rows_by, cols_by):
    rows, cols = lax.axis_size("ty"), lax.axis_size("tx")
    if not cols_by:
        return lax.ppermute(array, "ty", [(i, (i + rows_by) % rows) for i in range(rows)])
    if not rows_by:
        return lax.ppermute(array, "tx", [(i, (i + cols_by) % cols) for i in range(cols)])
    pairs = [
        (a * cols + b, (a + rows_by) % rows * cols + (b + cols_by) % cols)
        for a in range(rows)
        for b in range(cols)
    ]
    return lax.ppermute(array, ("ty", "tx"), pairs)


def swapped(array, axis, bit):
    length = lax.axis_size(axis)
    return lax.ppermute(array, axis, [(i, i ^ bit) for i in range(length)])


def picked(array, index):
    return lax.dynamic_index_in_dim(array, index, 0, keepdims=False)


def scattered(part, axis, unit, ways):
    me = (lax.axis_index(axis) // unit) % ways
    blocks = part.reshape(ways, -1, part.shape[-1])
    others = [swapped(picked(blocks, me ^ d), axis, d * unit) for d in range(1, ways)]
    return functools.reduce(jnp.add, others, picked(blocks, me))


def gathered(part, axis, unit, ways):
    me = (lax.axis_index(axis) // unit) % ways
    out = jnp.zeros((ways,) + part.shape, part.dtype)
    out = lax.dynamic_update_index_in_dim(out, part, me, 0)
    for d in range(1, ways):
        out = lax.dynamic_update_index_in_dim(out, swapped(part, axis, d * unit), me ^ d, 0)
    return out.reshape(-1, part.shape[-1])


def real_form(table):
    right = np.block([[table.real, table.imag], [-table.imag, table.real]]).astype(np.float32)
    high = right.astype(BF16)
    low = (right - high.astype(np.float32)).astype(BF16)
    return np.stack([high, low])


def tables(size):
    positions = np.arange(size)
    dft = np.exp(-2j * np.pi * (positions[:, None] * positions[None, :] % size) / size) / np.sqrt(size)
    freq = (positions + size // 2) % size - size // 2
    chirp = np.exp(-2j * np.pi * (freq * freq % (4 * size)) / (4 * size))
    through = dft.conj() @ (chirp[:, None] * dft)
    return np.stack([real_form(dft), real_form(through)])


def sided(pair):
    high, low = pair[0], pair[1]
    half = high.shape[0] // 2

    def turned(x):
        return jnp.concatenate(
            [jnp.concatenate([x[:half, :half], x[half:, :half]], axis=1),
             jnp.concatenate([x[:half, half:], x[half:, half:]], axis=1)], axis=0)

    left_high, left_low = turned(high), turned(low)
    return (
        jnp.concatenate([high, high, low], axis=0),
        jnp.concatenate([left_high, left_high, left_low], axis=1),
    )


def halves(x):
    high = x.astype(BF16)
    return high, (x - high.astype(F32)).astype(BF16)


def from_right(x, table):
    high, low = halves(x)
    return jnp.dot(jnp.concatenate([high, low, high], axis=1), table, preferred_element_type=F32)


def from_left(x, table):
    high, low = halves(x)
    return jnp.dot(table, jnp.concatenate([high, low, high], axis=0), preferred_element_type=F32)


def both_sides(fields, right_table, left_table):
    size = fields[0][0].shape[-1]
    done = []
    for first in range(0, len(fields), 2):
        pair = fields[first:first + 2]
        x = jnp.concatenate([jnp.concatenate(field, axis=1) for field in pair], axis=0)
        y = from_right(x, right_table)
        rows = [y[k * size:(k + 1) * size] for k in range(len(pair))]
        y = jnp.concatenate(
            [jnp.concatenate([r[:, :size], r[:, size:]], axis=0) for r in rows], axis=1
        )
        z = from_left(y, left_table)
        for k in range(len(pair)):
            lanes = slice(k * size, (k + 1) * size)
            done.append((z[:size, lanes], z[size:, lanes]))
    return done


def product(a, b):
    return (a[0] * b[0] - a[1] * b[1], a[0] * b[1] + a[1] * b[0])


def fill(wide, right, down, corner, size):
    wide[:, :size, size:] = right[...]
    wide[:, size:, :size] = down[...]
    wide[:, size:, size:] = corner[...]


SUBLANES = 8


def window_of(wide, at, slot, size):
    row, col = at[0, 0, 0, slot], at[1, 0, 0, slot]
    shift = lax.rem(row, SUBLANES)
    rows = pl.ds(pl.multiple_of(row - shift, SUBLANES), size + SUBLANES)
    left = lax.rem(2 * size - col, 2 * size)
    up = lax.rem(size + SUBLANES - shift, size + SUBLANES)
    return [
        pltpu.roll(pltpu.roll(wide[c, rows, :], left, axis=1)[:, :size], up, axis=0)[:size]
        for c in range(2)
    ]


def add_window(total, at, slot, grads, size):
    row, col = at[0, 0, 0, slot], at[1, 0, 0, slot]
    shift = lax.rem(row, SUBLANES)
    rows = pl.ds(pl.multiple_of(row - shift, SUBLANES), size + SUBLANES)
    for c in range(2):
        taller = jnp.concatenate([grads[c], jnp.zeros((SUBLANES, size), F32)], axis=0)
        lowered = pltpu.roll(taller, shift, axis=0)
        padded = jnp.concatenate([lowered, jnp.zeros_like(lowered)], axis=1)
        total[c, rows, :] += pltpu.roll(padded, col, axis=1)


def first_kernel(at_in, tile, probe_in, table_in, measured_in, right, down, corner,
                 psi, window, at_out, own, probe, table, measured, at, wide, sems):
    size = right.shape[-1]
    slots, modes = psi.shape[:2]
    soon = [(at_in, at), (tile.at[0], wide.at[:, pl.ds(0, size), pl.ds(0, size)]), (probe_in, probe),
            (table_in, table)]
    later = [(tile.at[1], own), (measured_in, measured), (at_in, at_out)]
    copies = [pltpu.make_async_copy(a, b, sems.at[i]) for i, (a, b) in enumerate(soon + later)]
    for copy in copies:
        copy.start()
    fill(wide, right, down.at[0], corner, size)
    for copy in copies[:len(soon)]:
        copy.wait()
    fields = []
    for slot in range(slots):
        w = window_of(wide, at, slot, size)
        window[slot, 0], window[slot, 1] = w
        fields += [product((probe[m, 0], probe[m, 1]), w) for m in range(modes)]
    waves = both_sides(fields, *sided(table[1]))
    for i, wave in enumerate(waves):
        psi[i // modes, i % modes, 0], psi[i // modes, i % modes, 1] = wave
    for copy in copies[len(soon):]:
        copy.wait()


def second_kernel(at, count, own, right, down, corner, psi, window, probe, measured, table,
                  g_probe, g_upper, g_lower, wide, total):
    size = own.shape[-1]
    slots, modes = psi.shape[:2]
    wide[:, :size, :size] = own[...]
    fill(wide, right, down.at[1], corner, size)
    total[...] = jnp.zeros_like(total)
    dft, through = sided(table[0]), sided(table[1])
    w = [window_of(wide, at, slot, size) for slot in range(slots)]
    waves = [[(psi[s, m, 0], psi[s, m, 1]) for m in range(modes)] for s in range(slots)]
    fields = [product(waves[s][m], w[s]) for s in range(slots) for m in range(modes)]
    far = both_sides(fields, *dft)
    fields = []
    for s in range(slots):
        own_far = far[s * modes:(s + 1) * modes]
        intensity = sum(re * re + im * im for re, im in own_far)
        live = jnp.where(s < count[0, 0], 2.0, 0.0).astype(F32)
        diff = (intensity - measured[s]) * live
        fields += [(re * diff, -(im * diff)) for re, im in own_far]
    conj = both_sides(fields, *dft)
    fields = [product(conj[s * modes + m], w[s]) for s in range(slots) for m in range(modes)]
    start = both_sides(fields, *through)
    for m in range(modes):
        parts = [product(start[s * modes + m], (window[s, 0], window[s, 1])) for s in range(slots)]
        g_probe[m, 0] = sum(re for re, _ in parts)
        g_probe[m, 1] = -sum(im for _, im in parts)
    for s in range(slots):
        for layer, (grads, by) in enumerate((
            (start, [(probe[m, 0], probe[m, 1]) for m in range(modes)]),
            (conj, waves[s]),
        )):
            parts = [product(grads[s * modes + m], by[m]) for m in range(modes)]
            pair = (sum(re for re, _ in parts), -sum(im for _, im in parts))
            add_window(total.at[layer], at, s, pair, size)
    g_upper[...] = total[:, :, :size, :]
    g_lower[...] = total[:, :, size:, :]


VMEM = pl.BlockSpec(memory_space=pltpu.VMEM)
SMEM = pl.BlockSpec(memory_space=pltpu.SMEM)
HBM = pl.BlockSpec(memory_space=pltpu.HBM)


def call(kernel, args, in_specs, outs, scratch, flops):
    args = [
        pltpu.with_memory_space_constraint(a, pltpu.HBM) if spec is HBM else a
        for a, spec in zip(args, in_specs)
    ]
    return pl.pallas_call(
        kernel,
        in_specs=in_specs,
        out_specs=[VMEM] * len(outs),
        out_shape=outs,
        scratch_shapes=scratch,
        compiler_params=pltpu.CompilerParams(vmem_limit_bytes=40 * 1024 * 1024),
        cost_estimate=pl.CostEstimate(flops=flops, bytes_accessed=4 * 1024 * 1024, transcendentals=0),
    )(*args)


def shaped(shape, dtype=F32):
    return jax.ShapeDtypeStruct(shape, dtype)


def on_device(object_slices, probe, measured, offsets, counts):
    layers, _, _, size = object_slices.shape
    slots = offsets.shape[-1]
    modes = probe.shape[0]
    measured = measured.reshape(slots, size, size)
    table = jnp.asarray(tables(size))
    flops = slots * modes * 2 * size * (2 * size) * (6 * size) * 2
    wide = pltpu.VMEM((2, 2 * size, 2 * size), F32)

    right_0 = moved(object_slices[0], 0, -1)
    corner_0 = moved(object_slices[0], -1, -1)
    down = moved(object_slices, -1, 0)
    right_1 = moved(object_slices[1], 0, -1)
    corner_1 = moved(object_slices[1], -1, -1)

    psi, window, at, own, *rest = call(
        first_kernel,
        (offsets, object_slices, probe, table, measured, right_0, down, corner_0),
        [HBM] * 5 + [VMEM] * 3,
        [shaped((slots, modes, 2, size, size)), shaped((slots, 2, size, size)), shaped(offsets.shape, jnp.int32),
         shaped((2, size, size)), shaped(probe.shape), shaped(table.shape, BF16), shaped(measured.shape)],
        [pltpu.SMEM(offsets.shape, jnp.int32), wide, pltpu.SemaphoreType.DMA((7,))], flops,
    )
    probe_near, table_near, measured_near = rest
    g_probe, g_upper, g_lower = call(
        second_kernel,
        (at, counts, own, right_1, down, corner_1, psi, window, probe_near, measured_near, table_near),
        [SMEM] * 2 + [VMEM] * 9,
        [shaped(probe.shape)] + [shaped((layers, 2, size, 2 * size))] * 2,
        [wide, pltpu.VMEM((layers, 2, 2 * size, 2 * size), F32)], 3 * flops,
    )

    rows = lax.axis_size("ty")
    part = scattered(g_probe.reshape(-1, size), "ty", 1, 2)
    part = scattered(part, "ty", 2, rows // 2)
    part, g_lower = lax.optimization_barrier((part, g_lower))
    from_above = moved(g_lower, 1, 0)
    bit = 1
    while bit < lax.axis_size("tx"):
        part = part + swapped(part, "tx", bit)
        bit *= 2
    g_wide = g_upper + from_above
    g_right, part = lax.optimization_barrier((g_wide[..., size:], part))
    from_left_tile = moved(g_right, 0, 1)
    part = gathered(part, "ty", 2, rows // 2)
    part = gathered(part, "ty", 1, 2)
    object_grad = g_wide[..., :size] + from_left_tile
    return object_grad, part.reshape(probe.shape)


def solution(mesh):
    in_specs = (
        P(None, None, "ty", "tx"),
        P(),
        P("ty", "tx", None, None, None),
        P(None, "ty", "tx", None),
        P("ty", "tx"),
    )
    out_specs = (P(None, None, "ty", "tx"), P())
    return jax.shard_map(
        on_device, mesh=mesh, in_specs=in_specs, out_specs=out_specs, check_vma=False
    )
```

```python
import functools

import jax
import jax.numpy as jnp
import numpy as np
from jax import lax
from jax.experimental import pallas as pl
from jax.experimental.pallas import tpu as pltpu
from jax.sharding import PartitionSpec as P

BF16 = jnp.bfloat16
F32 = jnp.float32


def moved(array, axis, by):
    length = lax.axis_size(axis)
    return lax.ppermute(array, axis, [(i, (i + by) % length) for i in range(length)])


def from_corner(array):
    rows, cols = lax.axis_size("ty"), lax.axis_size("tx")

    def target(a, b):
        if a > 0 and b > 0:
            return a - 1, b - 1
        if b > 0:
            return rows - 1, b
        return (a, cols - 1) if a < rows - 1 else (a, b)

    pairs = []
    for a in range(rows):
        for b in range(cols):
            down, over = target(a, b)
            pairs.append((a * cols + b, down * cols + over))
    return lax.ppermute(array, ("ty", "tx"), pairs)


def swapped(array, axis, bit):
    length = lax.axis_size(axis)
    return lax.ppermute(array, axis, [(i, i ^ bit) for i in range(length)])


def picked(array, index):
    return lax.dynamic_index_in_dim(array, index, 0, keepdims=False)


def scattered(part, axis, unit, ways):
    me = (lax.axis_index(axis) // unit) % ways
    blocks = part.reshape(ways, -1, part.shape[-1])
    others = [swapped(picked(blocks, me ^ d), axis, d * unit) for d in range(1, ways)]
    return functools.reduce(jnp.add, others, picked(blocks, me))


def gathered(part, axis, unit, ways):
    me = (lax.axis_index(axis) // unit) % ways
    out = jnp.zeros((ways,) + part.shape, part.dtype)
    out = lax.dynamic_update_index_in_dim(out, part, me, 0)
    for d in range(1, ways):
        out = lax.dynamic_update_index_in_dim(out, swapped(part, axis, d * unit), me ^ d, 0)
    return out.reshape(-1, part.shape[-1])


def real_form(table):
    right = np.block([[table.real, table.imag], [-table.imag, table.real]]).astype(np.float32)
    high = right.astype(BF16)
    low = (right - high.astype(np.float32)).astype(BF16)
    return np.stack([high, low])


def tables(size):
    positions = np.arange(size)
    dft = np.exp(-2j * np.pi * (positions[:, None] * positions[None, :] % size) / size) / np.sqrt(size)
    freq = (positions + size // 2) % size - size // 2
    chirp = np.exp(-2j * np.pi * (freq * freq % (4 * size)) / (4 * size))
    through = dft.conj() @ (chirp[:, None] * dft)
    return np.stack([real_form(dft), real_form(through)])


def sided(pair):
    high, low = pair[0], pair[1]
    half = high.shape[0] // 2

    def turned(x):
        return jnp.concatenate(
            [jnp.concatenate([x[:half, :half], x[half:, :half]], axis=1),
             jnp.concatenate([x[:half, half:], x[half:, half:]], axis=1)], axis=0)

    left_high, left_low = turned(high), turned(low)
    return (
        jnp.concatenate([high, high, low], axis=0),
        jnp.concatenate([left_high, left_high, left_low], axis=1),
    )


def halves(x):
    high = x.astype(BF16)
    return high, (x - high.astype(F32)).astype(BF16)


def from_right(x, table):
    high, low = halves(x)
    return jnp.dot(jnp.concatenate([high, low, high], axis=1), table, preferred_element_type=F32)


def from_left(x, table):
    high, low = halves(x)
    return jnp.dot(table, jnp.concatenate([high, low, high], axis=0), preferred_element_type=F32)


def both_sides(fields, right_table, left_table):
    size = fields[0][0].shape[-1]
    done = []
    for first in range(0, len(fields), 2):
        pair = fields[first:first + 2]
        x = jnp.concatenate([jnp.concatenate(field, axis=1) for field in pair], axis=0)
        y = from_right(x, right_table)
        rows = [y[k * size:(k + 1) * size] for k in range(len(pair))]
        y = jnp.concatenate(
            [jnp.concatenate([r[:, :size], r[:, size:]], axis=0) for r in rows], axis=1
        )
        z = from_left(y, left_table)
        for k in range(len(pair)):
            lanes = slice(k * size, (k + 1) * size)
            done.append((z[:size, lanes], z[size:, lanes]))
    return done


def product(a, b):
    return (a[0] * b[0] - a[1] * b[1], a[0] * b[1] + a[1] * b[0])


def fill(wide, right, down, corner, size):
    wide[:, :size, size:] = right[...]
    wide[:, size:, :size] = down[...]
    wide[:, size:, size:] = corner[...]


SUBLANES = 8


def window_of(wide, at, slot, size):
    row, col = at[0, 0, 0, slot], at[1, 0, 0, slot]
    shift = lax.rem(row, SUBLANES)
    rows = pl.ds(pl.multiple_of(row - shift, SUBLANES), size + SUBLANES)
    left = lax.rem(2 * size - col, 2 * size)
    up = lax.rem(size + SUBLANES - shift, size + SUBLANES)
    return [
        pltpu.roll(pltpu.roll(wide[c, rows, :], left, axis=1)[:, :size], up, axis=0)[:size]
        for c in range(2)
    ]


def add_window(total, at, slot, grads, size):
    row, col = at[0, 0, 0, slot], at[1, 0, 0, slot]
    shift = lax.rem(row, SUBLANES)
    rows = pl.ds(pl.multiple_of(row - shift, SUBLANES), size + SUBLANES)
    for c in range(2):
        taller = jnp.concatenate([grads[c], jnp.zeros((SUBLANES, size), F32)], axis=0)
        lowered = pltpu.roll(taller, shift, axis=0)
        padded = jnp.concatenate([lowered, jnp.zeros_like(lowered)], axis=1)
        total[c, rows, :] += pltpu.roll(padded, col, axis=1)


def first_kernel(at_in, tile, probe_in, table_in, measured_in, right, down, corner,
                 psi, window, at_out, own, probe, table, measured, at, wide, sems):
    size = right.shape[-1]
    slots, modes = psi.shape[:2]
    soon = [(at_in, at), (tile.at[0], wide.at[:, pl.ds(0, size), pl.ds(0, size)]), (probe_in, probe),
            (table_in, table)]
    later = [(tile.at[1], own), (measured_in, measured), (at_in, at_out)]
    copies = [pltpu.make_async_copy(a, b, sems.at[i]) for i, (a, b) in enumerate(soon + later)]
    for copy in copies:
        copy.start()
    fill(wide, right, down.at[0], corner, size)
    for copy in copies[:len(soon)]:
        copy.wait()
    fields = []
    for slot in range(slots):
        w = window_of(wide, at, slot, size)
        window[slot, 0], window[slot, 1] = w
        fields += [product((probe[m, 0], probe[m, 1]), w) for m in range(modes)]
    waves = both_sides(fields, *sided(table[1]))
    for i, wave in enumerate(waves):
        psi[i // modes, i % modes, 0], psi[i // modes, i % modes, 1] = wave
    for copy in copies[len(soon):]:
        copy.wait()


def second_kernel(at, count, own, right, down, corner, psi, window, probe, measured, table,
                  g_probe, g_upper, g_lower, wide, total):
    size = own.shape[-1]
    slots, modes = psi.shape[:2]
    wide[:, :size, :size] = own[...]
    fill(wide, right, down.at[1], corner, size)
    total[...] = jnp.zeros_like(total)
    dft, through = sided(table[0]), sided(table[1])
    w = [window_of(wide, at, slot, size) for slot in range(slots)]
    waves = [[(psi[s, m, 0], psi[s, m, 1]) for m in range(modes)] for s in range(slots)]
    fields = [product(waves[s][m], w[s]) for s in range(slots) for m in range(modes)]
    far = both_sides(fields, *dft)
    fields = []
    for s in range(slots):
        own_far = far[s * modes:(s + 1) * modes]
        intensity = sum(re * re + im * im for re, im in own_far)
        live = jnp.where(s < count[0, 0], 2.0, 0.0).astype(F32)
        diff = (intensity - measured[s]) * live
        fields += [(re * diff, -(im * diff)) for re, im in own_far]
    conj = both_sides(fields, *dft)
    fields = [product(conj[s * modes + m], w[s]) for s in range(slots) for m in range(modes)]
    start = both_sides(fields, *through)
    for m in range(modes):
        parts = [product(start[s * modes + m], (window[s, 0], window[s, 1])) for s in range(slots)]
        g_probe[m, 0] = sum(re for re, _ in parts)
        g_probe[m, 1] = -sum(im for _, im in parts)
    for s in range(slots):
        for layer, (grads, by) in enumerate((
            (start, [(probe[m, 0], probe[m, 1]) for m in range(modes)]),
            (conj, waves[s]),
        )):
            parts = [product(grads[s * modes + m], by[m]) for m in range(modes)]
            pair = (sum(re for re, _ in parts), -sum(im for _, im in parts))
            add_window(total.at[layer], at, s, pair, size)
    g_upper[...] = total[:, :, :size, :]
    g_lower[...] = total[:, :, size:, :]


VMEM = pl.BlockSpec(memory_space=pltpu.VMEM)
SMEM = pl.BlockSpec(memory_space=pltpu.SMEM)
HBM = pl.BlockSpec(memory_space=pltpu.HBM)


def call(kernel, args, in_specs, outs, scratch, flops):
    args = [
        pltpu.with_memory_space_constraint(a, pltpu.HBM) if spec is HBM else a
        for a, spec in zip(args, in_specs)
    ]
    return pl.pallas_call(
        kernel,
        in_specs=in_specs,
        out_specs=[VMEM] * len(outs),
        out_shape=outs,
        scratch_shapes=scratch,
        compiler_params=pltpu.CompilerParams(vmem_limit_bytes=40 * 1024 * 1024),
        cost_estimate=pl.CostEstimate(flops=flops, bytes_accessed=4 * 1024 * 1024, transcendentals=0),
    )(*args)


def shaped(shape, dtype=F32):
    return jax.ShapeDtypeStruct(shape, dtype)


def on_device(object_slices, probe, measured, offsets, counts):
    layers, _, _, size = object_slices.shape
    slots = offsets.shape[-1]
    modes = probe.shape[0]
    measured = measured.reshape(slots, size, size)
    table = jnp.asarray(tables(size))
    flops = slots * modes * 2 * size * (2 * size) * (6 * size) * 2
    wide = pltpu.VMEM((2, 2 * size, 2 * size), F32)

    right_0 = moved(object_slices[0], "tx", -1)
    corner_0 = from_corner(object_slices[0])
    down = moved(object_slices, "ty", -1)
    right_1 = moved(object_slices[1], "tx", -1)
    corner_1 = from_corner(object_slices[1])

    psi, window, at, own, *rest = call(
        first_kernel,
        (offsets, object_slices, probe, table, measured, right_0, down, corner_0),
        [HBM] * 5 + [VMEM] * 3,
        [shaped((slots, modes, 2, size, size)), shaped((slots, 2, size, size)), shaped(offsets.shape, jnp.int32),
         shaped((2, size, size)), shaped(probe.shape), shaped(table.shape, BF16), shaped(measured.shape)],
        [pltpu.SMEM(offsets.shape, jnp.int32), wide, pltpu.SemaphoreType.DMA((7,))], flops,
    )
    probe_near, table_near, measured_near = rest
    g_probe, g_upper, g_lower = call(
        second_kernel,
        (at, counts, own, right_1, down, corner_1, psi, window, probe_near, measured_near, table_near),
        [SMEM] * 2 + [VMEM] * 9,
        [shaped(probe.shape)] + [shaped((layers, 2, size, 2 * size))] * 2,
        [wide, pltpu.VMEM((layers, 2, 2 * size, 2 * size), F32)], 3 * flops,
    )

    rows = lax.axis_size("ty")
    part = scattered(g_probe.reshape(-1, size), "ty", 1, 2)
    part = scattered(part, "ty", 2, rows // 2)
    part, g_lower = lax.optimization_barrier((part, g_lower))
    from_above = moved(g_lower, "ty", 1)
    bit = 1
    while bit < lax.axis_size("tx"):
        part = part + swapped(part, "tx", bit)
        bit *= 2
    g_wide = g_upper + from_above
    g_right, part = lax.optimization_barrier((g_wide[..., size:], part))
    from_left_tile = moved(g_right, "tx", 1)
    part = gathered(part, "ty", 2, rows // 2)
    part = gathered(part, "ty", 1, 2)
    object_grad = g_wide[..., :size] + from_left_tile
    return object_grad, part.reshape(probe.shape)


def solution(mesh):
    in_specs = (
        P(None, None, "ty", "tx"),
        P(),
        P("ty", "tx", None, None, None),
        P(None, "ty", "tx", None),
        P("ty", "tx"),
    )
    out_specs = (P(None, None, "ty", "tx"), P())
    return jax.shard_map(
        on_device, mesh=mesh, in_specs=in_specs, out_specs=out_specs, check_vma=False
    )
```

```python
import functools

import jax
import jax.numpy as jnp
import numpy as np
from jax import lax
from jax.experimental import pallas as pl
from jax.experimental.pallas import tpu as pltpu
from jax.sharding import PartitionSpec as P

BF16 = jnp.bfloat16
F32 = jnp.float32


def moved(array, axis, by):
    length = lax.axis_size(axis)
    return lax.ppermute(array, axis, [(i, (i + by) % length) for i in range(length)])


def from_corner(array):
    rows, cols = lax.axis_size("ty"), lax.axis_size("tx")

    def target(a, b):
        if a > 0 and b > 0:
            return a - 1, b - 1
        if a == 0:
            return (rows - 1, b) if b < cols - 1 else (1, b)
        return (a if a > 1 else 0), cols - 1

    pairs = []
    for a in range(rows):
        for b in range(cols):
            down, over = target(a, b)
            pairs.append((a * cols + b, down * cols + over))
    return lax.ppermute(array, ("ty", "tx"), pairs)


def moved_open(array, axis, by):
    length = lax.axis_size(axis)
    return lax.ppermute(array, axis, [(i, i + by) for i in range(length) if 0 <= i + by < length])


def corner_open(array):
    rows, cols = lax.axis_size("ty"), lax.axis_size("tx")
    pairs = [(a * cols + b, (a - 1) * cols + b - 1) for a in range(1, rows) for b in range(1, cols)]
    return lax.ppermute(array, ("ty", "tx"), pairs)


def swapped(array, axis, bit):
    length = lax.axis_size(axis)
    return lax.ppermute(array, axis, [(i, i ^ bit) for i in range(length)])


def picked(array, index):
    return lax.dynamic_index_in_dim(array, index, 0, keepdims=False)


def scattered(part, axis, unit, ways):
    me = (lax.axis_index(axis) // unit) % ways
    blocks = part.reshape(ways, -1, part.shape[-1])
    others = [swapped(picked(blocks, me ^ d), axis, d * unit) for d in range(1, ways)]
    return functools.reduce(jnp.add, others, picked(blocks, me))


def gathered(part, axis, unit, ways):
    me = (lax.axis_index(axis) // unit) % ways
    out = jnp.zeros((ways,) + part.shape, part.dtype)
    out = lax.dynamic_update_index_in_dim(out, part, me, 0)
    for d in range(1, ways):
        out = lax.dynamic_update_index_in_dim(out, swapped(part, axis, d * unit), me ^ d, 0)
    return out.reshape(-1, part.shape[-1])


def real_form(table):
    right = np.block([[table.real, table.imag], [-table.imag, table.real]]).astype(np.float32)
    high = right.astype(BF16)
    low = (right - high.astype(np.float32)).astype(BF16)
    return np.stack([high, low])


def tables(size):
    positions = np.arange(size)
    dft = np.exp(-2j * np.pi * (positions[:, None] * positions[None, :] % size) / size) / np.sqrt(size)
    freq = (positions + size // 2) % size - size // 2
    chirp = np.exp(-2j * np.pi * (freq * freq % (4 * size)) / (4 * size))
    through = dft.conj() @ (chirp[:, None] * dft)
    return np.stack([real_form(dft), real_form(through)])


def sided(pair):
    high, low = pair[0], pair[1]
    half = high.shape[0] // 2

    def turned(x):
        return jnp.concatenate(
            [jnp.concatenate([x[:half, :half], x[half:, :half]], axis=1),
             jnp.concatenate([x[:half, half:], x[half:, half:]], axis=1)], axis=0)

    left_high, left_low = turned(high), turned(low)
    return (
        jnp.concatenate([high, high, low], axis=0),
        jnp.concatenate([left_high, left_high, left_low], axis=1),
    )


def halves(x):
    high = x.astype(BF16)
    return high, (x - high.astype(F32)).astype(BF16)


def from_right(x, table):
    high, low = halves(x)
    return jnp.dot(jnp.concatenate([high, low, high], axis=1), table, preferred_element_type=F32)


def from_left(x, table):
    high, low = halves(x)
    return jnp.dot(table, jnp.concatenate([high, low, high], axis=0), preferred_element_type=F32)


def both_sides(fields, right_table, left_table):
    size = fields[0][0].shape[-1]
    done = []
    for first in range(0, len(fields), 2):
        pair = fields[first:first + 2]
        x = jnp.concatenate([jnp.concatenate(field, axis=1) for field in pair], axis=0)
        y = from_right(x, right_table)
        rows = [y[k * size:(k + 1) * size] for k in range(len(pair))]
        y = jnp.concatenate(
            [jnp.concatenate([r[:, :size], r[:, size:]], axis=0) for r in rows], axis=1
        )
        z = from_left(y, left_table)
        for k in range(len(pair)):
            lanes = slice(k * size, (k + 1) * size)
            done.append((z[:size, lanes], z[size:, lanes]))
    return done


def product(a, b):
    return (a[0] * b[0] - a[1] * b[1], a[0] * b[1] + a[1] * b[0])


def fill(wide, right, down, corner, size):
    wide[:, :size, size:] = right[...]
    wide[:, size:, :size] = down[...]
    wide[:, size:, size:] = corner[...]


SUBLANES = 8


def window_of(wide, at, slot, size):
    row, col = at[0, 0, 0, slot], at[1, 0, 0, slot]
    shift = lax.rem(row, SUBLANES)
    rows = pl.ds(pl.multiple_of(row - shift, SUBLANES), size + SUBLANES)
    left = lax.rem(2 * size - col, 2 * size)
    up = lax.rem(size + SUBLANES - shift, size + SUBLANES)
    return [
        pltpu.roll(pltpu.roll(wide[c, rows, :], left, axis=1)[:, :size], up, axis=0)[:size]
        for c in range(2)
    ]


def add_window(total, at, slot, grads, size):
    row, col = at[0, 0, 0, slot], at[1, 0, 0, slot]
    shift = lax.rem(row, SUBLANES)
    rows = pl.ds(pl.multiple_of(row - shift, SUBLANES), size + SUBLANES)
    for c in range(2):
        taller = jnp.concatenate([grads[c], jnp.zeros((SUBLANES, size), F32)], axis=0)
        lowered = pltpu.roll(taller, shift, axis=0)
        padded = jnp.concatenate([lowered, jnp.zeros_like(lowered)], axis=1)
        total[c, rows, :] += pltpu.roll(padded, col, axis=1)


def first_kernel(at_in, tile, probe_in, table_in, measured_in, right, down, corner,
                 psi, window, at_out, own, probe, table, measured, at, wide, sems):
    size = right.shape[-1]
    slots, modes = psi.shape[:2]
    soon = [(at_in, at), (tile.at[0], wide.at[:, pl.ds(0, size), pl.ds(0, size)]), (probe_in, probe),
            (table_in, table)]
    later = [(tile.at[1], own), (measured_in, measured), (at_in, at_out)]
    copies = [pltpu.make_async_copy(a, b, sems.at[i]) for i, (a, b) in enumerate(soon + later)]
    for copy in copies:
        copy.start()
    fill(wide, right, down.at[0], corner, size)
    for copy in copies[:len(soon)]:
        copy.wait()
    fields = []
    for slot in range(slots):
        w = window_of(wide, at, slot, size)
        window[slot, 0], window[slot, 1] = w
        fields += [product((probe[m, 0], probe[m, 1]), w) for m in range(modes)]
    waves = both_sides(fields, *sided(table[1]))
    for i, wave in enumerate(waves):
        psi[i // modes, i % modes, 0], psi[i // modes, i % modes, 1] = wave
    for copy in copies[len(soon):]:
        copy.wait()


def second_kernel(at, count, own, right, down, corner, psi, window, probe, measured, table,
                  g_probe, g_upper, g_lower, wide, total):
    size = own.shape[-1]
    slots, modes = psi.shape[:2]
    wide[:, :size, :size] = own[...]
    fill(wide, right, down.at[1], corner, size)
    total[...] = jnp.zeros_like(total)
    dft, through = sided(table[0]), sided(table[1])
    w = [window_of(wide, at, slot, size) for slot in range(slots)]
    waves = [[(psi[s, m, 0], psi[s, m, 1]) for m in range(modes)] for s in range(slots)]
    fields = [product(waves[s][m], w[s]) for s in range(slots) for m in range(modes)]
    far = both_sides(fields, *dft)
    fields = []
    for s in range(slots):
        own_far = far[s * modes:(s + 1) * modes]
        intensity = sum(re * re + im * im for re, im in own_far)
        live = jnp.where(s < count[0, 0], 2.0, 0.0).astype(F32)
        diff = (intensity - measured[s]) * live
        fields += [(re * diff, -(im * diff)) for re, im in own_far]
    conj = both_sides(fields, *dft)
    fields = [product(conj[s * modes + m], w[s]) for s in range(slots) for m in range(modes)]
    start = both_sides(fields, *through)
    for m in range(modes):
        parts = [product(start[s * modes + m], (window[s, 0], window[s, 1])) for s in range(slots)]
        g_probe[m, 0] = sum(re for re, _ in parts)
        g_probe[m, 1] = -sum(im for _, im in parts)
    for s in range(slots):
        for layer, (grads, by) in enumerate((
            (start, [(probe[m, 0], probe[m, 1]) for m in range(modes)]),
            (conj, waves[s]),
        )):
            parts = [product(grads[s * modes + m], by[m]) for m in range(modes)]
            pair = (sum(re for re, _ in parts), -sum(im for _, im in parts))
            add_window(total.at[layer], at, s, pair, size)
    g_upper[...] = total[:, :, :size, :]
    g_lower[...] = total[:, :, size:, :]


VMEM = pl.BlockSpec(memory_space=pltpu.VMEM)
SMEM = pl.BlockSpec(memory_space=pltpu.SMEM)
HBM = pl.BlockSpec(memory_space=pltpu.HBM)


def call(kernel, args, in_specs, outs, scratch, flops):
    args = [
        pltpu.with_memory_space_constraint(a, pltpu.HBM) if spec is HBM else a
        for a, spec in zip(args, in_specs)
    ]
    return pl.pallas_call(
        kernel,
        in_specs=in_specs,
        out_specs=[VMEM] * len(outs),
        out_shape=outs,
        scratch_shapes=scratch,
        compiler_params=pltpu.CompilerParams(vmem_limit_bytes=40 * 1024 * 1024),
        cost_estimate=pl.CostEstimate(flops=flops, bytes_accessed=4 * 1024 * 1024, transcendentals=0),
    )(*args)


def shaped(shape, dtype=F32):
    return jax.ShapeDtypeStruct(shape, dtype)


def on_device(object_slices, probe, measured, offsets, counts):
    layers, _, _, size = object_slices.shape
    slots = offsets.shape[-1]
    modes = probe.shape[0]
    measured = measured.reshape(slots, size, size)
    table = jnp.asarray(tables(size))
    flops = slots * modes * 2 * size * (2 * size) * (6 * size) * 2
    wide = pltpu.VMEM((2, 2 * size, 2 * size), F32)

    right_0 = moved_open(object_slices[0], "tx", -1)
    corner_0 = from_corner(object_slices[0])
    down = moved(object_slices, "ty", -1)
    right_1 = moved_open(object_slices[1], "tx", -1)
    corner_1 = from_corner(object_slices[1])

    psi, window, at, own, *rest = call(
        first_kernel,
        (offsets, object_slices, probe, table, measured, right_0, down, corner_0),
        [HBM] * 5 + [VMEM] * 3,
        [shaped((slots, modes, 2, size, size)), shaped((slots, 2, size, size)), shaped(offsets.shape, jnp.int32),
         shaped((2, size, size)), shaped(probe.shape), shaped(table.shape, BF16), shaped(measured.shape)],
        [pltpu.SMEM(offsets.shape, jnp.int32), wide, pltpu.SemaphoreType.DMA((7,))], flops,
    )
    probe_near, table_near, measured_near = rest
    g_probe, g_upper, g_lower = call(
        second_kernel,
        (at, counts, own, right_1, down, corner_1, psi, window, probe_near, measured_near, table_near),
        [SMEM] * 2 + [VMEM] * 9,
        [shaped(probe.shape)] + [shaped((layers, 2, size, 2 * size))] * 2,
        [wide, pltpu.VMEM((layers, 2, 2 * size, 2 * size), F32)], 3 * flops,
    )

    rows = lax.axis_size("ty")
    part = scattered(g_probe.reshape(-1, size), "ty", 1, 2)
    part = scattered(part, "ty", 2, rows // 2)
    part, g_lower = lax.optimization_barrier((part, g_lower))
    from_above = moved(g_lower, "ty", 1)
    bit = 1
    while bit < lax.axis_size("tx"):
        part = part + swapped(part, "tx", bit)
        bit *= 2
    part, from_above = lax.optimization_barrier((part, from_above))
    g_wide = g_upper + from_above
    g_right, g_own = lax.optimization_barrier((g_wide[..., size:], g_wide[..., :size]))
    from_left_tile = moved(g_right, "tx", 1)
    part, g_right = lax.optimization_barrier((part, g_right))
    part = gathered(part, "ty", 2, rows // 2)
    part = gathered(part, "ty", 1, 2)
    object_grad = g_own + from_left_tile
    return object_grad, part.reshape(probe.shape)


def solution(mesh):
    in_specs = (
        P(None, None, "ty", "tx"),
        P(),
        P("ty", "tx", None, None, None),
        P(None, "ty", "tx", None),
        P("ty", "tx"),
    )
    out_specs = (P(None, None, "ty", "tx"), P())
    return jax.shard_map(
        on_device, mesh=mesh, in_specs=in_specs, out_specs=out_specs, check_vma=False
    )
```

```python
import functools

import jax
import jax.numpy as jnp
import numpy as np
from jax import lax
from jax.experimental import pallas as pl
from jax.experimental.pallas import tpu as pltpu
from jax.sharding import PartitionSpec as P

BF16 = jnp.bfloat16
F32 = jnp.float32


def moved(array, axis, by):
    length = lax.axis_size(axis)
    return lax.ppermute(array, axis, [(i, (i + by) % length) for i in range(length)])


def from_corner(array):
    rows, cols = lax.axis_size("ty"), lax.axis_size("tx")

    def target(a, b):
        if a > 0 and b > 0:
            return a - 1, b - 1
        if a == 0:
            return (rows - 1, b) if b < cols - 1 else (1, b)
        return (a if a > 1 else 0), cols - 1

    pairs = []
    for a in range(rows):
        for b in range(cols):
            down, over = target(a, b)
            pairs.append((a * cols + b, down * cols + over))
    return lax.ppermute(array, ("ty", "tx"), pairs)


def moved_open(array, axis, by):
    length = lax.axis_size(axis)
    return lax.ppermute(array, axis, [(i, i + by) for i in range(length) if 0 <= i + by < length])


def corner_open(array):
    rows, cols = lax.axis_size("ty"), lax.axis_size("tx")
    pairs = [(a * cols + b, (a - 1) * cols + b - 1) for a in range(1, rows) for b in range(1, cols)]
    return lax.ppermute(array, ("ty", "tx"), pairs)


def swapped(array, axis, bit):
    length = lax.axis_size(axis)
    return lax.ppermute(array, axis, [(i, i ^ bit) for i in range(length)])


def picked(array, index):
    return lax.dynamic_index_in_dim(array, index, 0, keepdims=False)


def scattered(part, axis, unit, ways):
    me = (lax.axis_index(axis) // unit) % ways
    blocks = part.reshape(ways, -1, part.shape[-1])
    others = [swapped(picked(blocks, me ^ d), axis, d * unit) for d in range(1, ways)]
    return functools.reduce(jnp.add, others, picked(blocks, me))


def gathered(part, axis, unit, ways):
    me = (lax.axis_index(axis) // unit) % ways
    out = jnp.zeros((ways,) + part.shape, part.dtype)
    out = lax.dynamic_update_index_in_dim(out, part, me, 0)
    for d in range(1, ways):
        out = lax.dynamic_update_index_in_dim(out, swapped(part, axis, d * unit), me ^ d, 0)
    return out.reshape(-1, part.shape[-1])


def real_form(table):
    right = np.block([[table.real, table.imag], [-table.imag, table.real]]).astype(np.float32)
    high = right.astype(BF16)
    low = (right - high.astype(np.float32)).astype(BF16)
    return np.stack([high, low])


def tables(size):
    positions = np.arange(size)
    dft = np.exp(-2j * np.pi * (positions[:, None] * positions[None, :] % size) / size) / np.sqrt(size)
    freq = (positions + size // 2) % size - size // 2
    chirp = np.exp(-2j * np.pi * (freq * freq % (4 * size)) / (4 * size))
    through = dft.conj() @ (chirp[:, None] * dft)
    return np.stack([real_form(dft), real_form(through)])


def sided(pair):
    high, low = pair[0], pair[1]
    half = high.shape[0] // 2

    def turned(x):
        return jnp.concatenate(
            [jnp.concatenate([x[:half, :half], x[half:, :half]], axis=1),
             jnp.concatenate([x[:half, half:], x[half:, half:]], axis=1)], axis=0)

    left_high, left_low = turned(high), turned(low)
    return (
        jnp.concatenate([high, high, low], axis=0),
        jnp.concatenate([left_high, left_high, left_low], axis=1),
    )


def halves(x):
    high = x.astype(BF16)
    return high, (x - high.astype(F32)).astype(BF16)


def from_right(x, table):
    high, low = halves(x)
    return jnp.dot(jnp.concatenate([high, low, high], axis=1), table, preferred_element_type=F32)


def from_left(x, table):
    high, low = halves(x)
    return jnp.dot(table, jnp.concatenate([high, low, high], axis=0), preferred_element_type=F32)


def both_sides(fields, right_table, left_table):
    size = fields[0][0].shape[-1]
    done = []
    for first in range(0, len(fields), 2):
        pair = fields[first:first + 2]
        x = jnp.concatenate([jnp.concatenate(field, axis=1) for field in pair], axis=0)
        y = from_right(x, right_table)
        rows = [y[k * size:(k + 1) * size] for k in range(len(pair))]
        y = jnp.concatenate(
            [jnp.concatenate([r[:, :size], r[:, size:]], axis=0) for r in rows], axis=1
        )
        z = from_left(y, left_table)
        for k in range(len(pair)):
            lanes = slice(k * size, (k + 1) * size)
            done.append((z[:size, lanes], z[size:, lanes]))
    return done


def product(a, b):
    return (a[0] * b[0] - a[1] * b[1], a[0] * b[1] + a[1] * b[0])


def fill(wide, own, right, down, corner, size):
    wide[:, :size, :size] = own[...]
    wide[:, :size, size:] = right[...]
    wide[:, size:, :size] = down[...]
    wide[:, size:, size:] = corner[...]


SUBLANES = 8


def window_of(wide, at, slot, size):
    row, col = at[0, 0, 0, slot], at[1, 0, 0, slot]
    shift = lax.rem(row, SUBLANES)
    rows = pl.ds(pl.multiple_of(row - shift, SUBLANES), size + SUBLANES)
    left = lax.rem(2 * size - col, 2 * size)
    up = lax.rem(size + SUBLANES - shift, size + SUBLANES)
    return [
        pltpu.roll(pltpu.roll(wide[c, rows, :], left, axis=1)[:, :size], up, axis=0)[:size]
        for c in range(2)
    ]


def add_window(total, at, slot, grads, size):
    row, col = at[0, 0, 0, slot], at[1, 0, 0, slot]
    shift = lax.rem(row, SUBLANES)
    rows = pl.ds(pl.multiple_of(row - shift, SUBLANES), size + SUBLANES)
    for c in range(2):
        taller = jnp.concatenate([grads[c], jnp.zeros((SUBLANES, size), F32)], axis=0)
        lowered = pltpu.roll(taller, shift, axis=0)
        padded = jnp.concatenate([lowered, jnp.zeros_like(lowered)], axis=1)
        total[c, rows, :] += pltpu.roll(padded, col, axis=1)


def near_kernel(*refs):
    count = (len(refs) - 1) // 2
    copies = [
        pltpu.make_async_copy(refs[i], refs[count + i], refs[-1].at[i]) for i in range(count)
    ]
    for copy in copies:
        copy.start()
    for copy in copies:
        copy.wait()


def first_kernel(at, tile, probe, table, right, down, corner, psi, window, wide):
    size = right.shape[-1]
    slots, modes = psi.shape[:2]
    fill(wide, tile.at[0], right, down.at[0], corner, size)
    fields = []
    for slot in range(slots):
        w = window_of(wide, at, slot, size)
        window[slot, 0], window[slot, 1] = w
        fields += [product((probe[m, 0], probe[m, 1]), w) for m in range(modes)]
    waves = both_sides(fields, *sided(table[1]))
    for i, wave in enumerate(waves):
        psi[i // modes, i % modes, 0], psi[i // modes, i % modes, 1] = wave


def second_kernel(at, count, tile, right, down, corner, psi, window, probe, measured, table,
                  g_probe, g_windows, wide):
    size = right.shape[-1]
    slots, modes = psi.shape[:2]
    fill(wide, tile.at[1], right, down.at[1], corner, size)
    dft, through = sided(table[0]), sided(table[1])
    w = [window_of(wide, at, slot, size) for slot in range(slots)]
    waves = [[(psi[s, m, 0], psi[s, m, 1]) for m in range(modes)] for s in range(slots)]
    fields = [product(waves[s][m], w[s]) for s in range(slots) for m in range(modes)]
    far = both_sides(fields, *dft)
    fields = []
    for s in range(slots):
        own_far = far[s * modes:(s + 1) * modes]
        intensity = sum(re * re + im * im for re, im in own_far)
        live = jnp.where(s < count[0, 0], 2.0, 0.0).astype(F32)
        diff = (intensity - measured[s]) * live
        fields += [(re * diff, -(im * diff)) for re, im in own_far]
    conj = both_sides(fields, *dft)
    fields = [product(conj[s * modes + m], w[s]) for s in range(slots) for m in range(modes)]
    start = both_sides(fields, *through)
    for m in range(modes):
        parts = [product(start[s * modes + m], (window[s, 0], window[s, 1])) for s in range(slots)]
        g_probe[m, 0] = sum(re for re, _ in parts)
        g_probe[m, 1] = -sum(im for _, im in parts)
    for s in range(slots):
        for layer, (grads, by) in enumerate((
            (start, [(probe[m, 0], probe[m, 1]) for m in range(modes)]),
            (conj, waves[s]),
        )):
            parts = [product(grads[s * modes + m], by[m]) for m in range(modes)]
            g_windows[layer, s, 0] = sum(re for re, _ in parts)
            g_windows[layer, s, 1] = -sum(im for _, im in parts)


def object_kernel(at, g_windows, g_upper, g_lower, total):
    layers, slots, _, size, _ = g_windows.shape
    total[...] = jnp.zeros_like(total)
    for s in range(slots):
        for layer in range(layers):
            add_window(total.at[layer], at, s, (g_windows[layer, s, 0], g_windows[layer, s, 1]), size)
    g_upper[...] = total[:, :, :size, :]
    g_lower[...] = total[:, :, size:, :]


VMEM = pl.BlockSpec(memory_space=pltpu.VMEM)
SMEM = pl.BlockSpec(memory_space=pltpu.SMEM)
HBM = pl.BlockSpec(memory_space=pltpu.HBM)


def call(kernel, args, in_specs, outs, scratch, flops):
    args = [
        pltpu.with_memory_space_constraint(a, pltpu.HBM) if spec is HBM else a
        for a, spec in zip(args, in_specs)
    ]
    return pl.pallas_call(
        kernel,
        in_specs=in_specs,
        out_specs=[VMEM] * len(outs),
        out_shape=outs,
        scratch_shapes=scratch,
        compiler_params=pltpu.CompilerParams(vmem_limit_bytes=24 * 1024 * 1024),
        cost_estimate=pl.CostEstimate(flops=flops, bytes_accessed=4 * 1024 * 1024, transcendentals=0),
    )(*args)


def shaped(shape, dtype=F32):
    return jax.ShapeDtypeStruct(shape, dtype)


def on_device(object_slices, probe, measured, offsets, counts):
    layers, _, _, size = object_slices.shape
    slots = offsets.shape[-1]
    modes = probe.shape[0]
    measured = measured.reshape(slots, size, size)
    table = jnp.asarray(tables(size))
    flops = slots * modes * 2 * size * (2 * size) * (6 * size) * 2
    wide = pltpu.VMEM((2, 2 * size, 2 * size), F32)

    right_0 = moved_open(object_slices[0], "tx", -1)
    right_1 = moved_open(object_slices[1], "tx", -1)
    down = moved(object_slices, "ty", -1)
    corner_0 = moved(right_0, "ty", -1)
    corner_1 = moved(right_1, "ty", -1)
    far = (offsets, object_slices, probe, table, measured)
    at, tile, probe_near, table_near, measured_near = call(
        near_kernel, far, [HBM] * len(far), [shaped(a.shape, a.dtype) for a in far],
        [pltpu.SemaphoreType.DMA((len(far),))], flops,
    )
    psi, window = call(
        first_kernel,
        (at, tile, probe_near, table_near, right_0, down, corner_0),
        [SMEM] + [VMEM] * 6,
        [shaped((slots, modes, 2, size, size)), shaped((slots, 2, size, size))],
        [wide], flops,
    )
    g_probe, g_windows = call(
        second_kernel,
        (at, counts, tile, right_1, down, corner_1, psi, window, probe_near, measured_near, table_near),
        [SMEM] * 2 + [VMEM] * 9,
        [shaped(probe.shape), shaped((layers, slots, 2, size, size))],
        [wide], 3 * flops,
    )

    rows = lax.axis_size("ty")
    part = scattered(g_probe.reshape(-1, size), "ty", 1, 2)
    part, g_windows = lax.optimization_barrier((part, g_windows))
    part = scattered(part, "ty", 2, rows // 2)
    g_upper, g_lower = call(
        object_kernel, (at, g_windows), [SMEM, VMEM],
        [shaped((layers, 2, size, 2 * size))] * 2,
        [pltpu.VMEM((layers, 2, 2 * size, 2 * size), F32)], flops // 4,
    )
    part, g_lower = lax.optimization_barrier((part, g_lower))
    from_above = moved(g_lower, "ty", 1)
    bit = 1
    while bit < lax.axis_size("tx"):
        part = part + swapped(part, "tx", bit)
        bit *= 2
    part, from_above = lax.optimization_barrier((part, from_above))
    g_wide = g_upper + from_above
    g_right, g_own = lax.optimization_barrier((g_wide[..., size:], g_wide[..., :size]))
    from_left_tile = moved(g_right, "tx", 1)
    part, g_right = lax.optimization_barrier((part, g_right))
    part = gathered(part, "ty", 2, rows // 2)
    part = gathered(part, "ty", 1, 2)
    object_grad = g_own + from_left_tile
    return object_grad, part.reshape(probe.shape)


def solution(mesh):
    in_specs = (
        P(None, None, "ty", "tx"),
        P(),
        P("ty", "tx", None, None, None),
        P(None, "ty", "tx", None),
        P("ty", "tx"),
    )
    out_specs = (P(None, None, "ty", "tx"), P())
    return jax.shard_map(
        on_device, mesh=mesh, in_specs=in_specs, out_specs=out_specs, check_vma=False
    )
```

```python
import functools

import jax
import jax.numpy as jnp
import numpy as np
from jax import lax
from jax.experimental import pallas as pl
from jax.experimental.pallas import tpu as pltpu
from jax.sharding import PartitionSpec as P

BF16 = jnp.bfloat16
F32 = jnp.float32


def moved(array, axis, by):
    length = lax.axis_size(axis)
    return lax.ppermute(array, axis, [(i, (i + by) % length) for i in range(length)])


def from_corner(array):
    rows, cols = lax.axis_size("ty"), lax.axis_size("tx")

    def target(a, b):
        if a > 0 and b > 0:
            return a - 1, b - 1
        if a == 0:
            return (rows - 1, b) if b < cols - 1 else (1, b)
        return (a if a > 1 else 0), cols - 1

    pairs = []
    for a in range(rows):
        for b in range(cols):
            down, over = target(a, b)
            pairs.append((a * cols + b, down * cols + over))
    return lax.ppermute(array, ("ty", "tx"), pairs)


def moved_open(array, axis, by):
    length = lax.axis_size(axis)
    return lax.ppermute(array, axis, [(i, i + by) for i in range(length) if 0 <= i + by < length])


def corner_open(array):
    rows, cols = lax.axis_size("ty"), lax.axis_size("tx")
    pairs = [(a * cols + b, (a - 1) * cols + b - 1) for a in range(1, rows) for b in range(1, cols)]
    return lax.ppermute(array, ("ty", "tx"), pairs)


def swapped(array, axis, bit):
    length = lax.axis_size(axis)
    return lax.ppermute(array, axis, [(i, i ^ bit) for i in range(length)])


def picked(array, index):
    return lax.dynamic_index_in_dim(array, index, 0, keepdims=False)


def scattered(part, axis, unit, ways):
    me = (lax.axis_index(axis) // unit) % ways
    blocks = part.reshape(ways, -1, part.shape[-1])
    others = [swapped(picked(blocks, me ^ d), axis, d * unit) for d in range(1, ways)]
    return functools.reduce(jnp.add, others, picked(blocks, me))


def gathered(part, axis, unit, ways):
    me = (lax.axis_index(axis) // unit) % ways
    out = jnp.zeros((ways,) + part.shape, part.dtype)
    out = lax.dynamic_update_index_in_dim(out, part, me, 0)
    for d in range(ways - 1, 0, -1):
        out = lax.dynamic_update_index_in_dim(out, swapped(part, axis, d * unit), me ^ d, 0)
    return out.reshape(-1, part.shape[-1])


def real_form(table):
    right = np.block([[table.real, table.imag], [-table.imag, table.real]]).astype(np.float32)
    high = right.astype(BF16)
    low = (right - high.astype(np.float32)).astype(BF16)
    return np.stack([high, low])


def tables(size):
    positions = np.arange(size)
    dft = np.exp(-2j * np.pi * (positions[:, None] * positions[None, :] % size) / size) / np.sqrt(size)
    freq = (positions + size // 2) % size - size // 2
    chirp = np.exp(-2j * np.pi * (freq * freq % (4 * size)) / (4 * size))
    through = dft.conj() @ (chirp[:, None] * dft)
    return np.stack([real_form(dft), real_form(through)])


def sided(pair):
    high, low = pair[0], pair[1]
    half = high.shape[0] // 2

    def turned(x):
        return jnp.concatenate(
            [jnp.concatenate([x[:half, :half], x[half:, :half]], axis=1),
             jnp.concatenate([x[:half, half:], x[half:, half:]], axis=1)], axis=0)

    left_high, left_low = turned(high), turned(low)
    return (
        jnp.concatenate([high, high, low], axis=0),
        jnp.concatenate([left_high, left_high, left_low], axis=1),
    )


def halves(x):
    high = x.astype(BF16)
    return high, (x - high.astype(F32)).astype(BF16)


def from_right(x, table):
    high, low = halves(x)
    return jnp.dot(jnp.concatenate([high, low, high], axis=1), table, preferred_element_type=F32)


def from_left(x, table):
    high, low = halves(x)
    return jnp.dot(table, jnp.concatenate([high, low, high], axis=0), preferred_element_type=F32)


def both_sides(fields, right_table, left_table):
    size = fields[0][0].shape[-1]
    done = []
    for first in range(0, len(fields), 2):
        pair = fields[first:first + 2]
        x = jnp.concatenate([jnp.concatenate(field, axis=1) for field in pair], axis=0)
        y = from_right(x, right_table)
        rows = [y[k * size:(k + 1) * size] for k in range(len(pair))]
        y = jnp.concatenate(
            [jnp.concatenate([r[:, :size], r[:, size:]], axis=0) for r in rows], axis=1
        )
        z = from_left(y, left_table)
        for k in range(len(pair)):
            lanes = slice(k * size, (k + 1) * size)
            done.append((z[:size, lanes], z[size:, lanes]))
    return done


def product(a, b):
    return (a[0] * b[0] - a[1] * b[1], a[0] * b[1] + a[1] * b[0])


def fill(wide, own, right, down, corner, size):
    wide[:, :size, :size] = own[...]
    wide[:, :size, size:] = right[...]
    wide[:, size:, :size] = down[...]
    wide[:, size:, size:] = corner[...]


SUBLANES = 8


def window_of(wide, at, slot, size):
    row, col = at[0, 0, 0, slot], at[1, 0, 0, slot]
    shift = lax.rem(row, SUBLANES)
    rows = pl.ds(pl.multiple_of(row - shift, SUBLANES), size + SUBLANES)
    left = lax.rem(2 * size - col, 2 * size)
    up = lax.rem(size + SUBLANES - shift, size + SUBLANES)
    return [
        pltpu.roll(pltpu.roll(wide[c, rows, :], left, axis=1)[:, :size], up, axis=0)[:size]
        for c in range(2)
    ]


def add_window(total, at, slot, grads, size):
    row, col = at[0, 0, 0, slot], at[1, 0, 0, slot]
    shift = lax.rem(row, SUBLANES)
    rows = pl.ds(pl.multiple_of(row - shift, SUBLANES), size + SUBLANES)
    for c in range(2):
        taller = jnp.concatenate([grads[c], jnp.zeros((SUBLANES, size), F32)], axis=0)
        lowered = pltpu.roll(taller, shift, axis=0)
        padded = jnp.concatenate([lowered, jnp.zeros_like(lowered)], axis=1)
        total[c, rows, :] += pltpu.roll(padded, col, axis=1)


def near_kernel(*refs):
    count = (len(refs) - 1) // 2
    copies = [
        pltpu.make_async_copy(refs[i], refs[count + i], refs[-1].at[i]) for i in range(count)
    ]
    for copy in copies:
        copy.start()
    for copy in copies:
        copy.wait()


def first_kernel(at, tile, probe, table, right, down, corner, psi, window, wide):
    size = right.shape[-1]
    slots, modes = psi.shape[:2]
    fill(wide, tile.at[0], right, down.at[0], corner, size)
    fields = []
    for slot in range(slots):
        w = window_of(wide, at, slot, size)
        window[slot, 0], window[slot, 1] = w
        fields += [product((probe[m, 0], probe[m, 1]), w) for m in range(modes)]
    waves = both_sides(fields, *sided(table[1]))
    for i, wave in enumerate(waves):
        psi[i // modes, i % modes, 0], psi[i // modes, i % modes, 1] = wave


def second_kernel(at, count, tile, right, down, corner, psi, window, probe, measured, table,
                  g_probe, g_windows, wide):
    size = right.shape[-1]
    slots, modes = psi.shape[:2]
    fill(wide, tile.at[1], right, down.at[1], corner, size)
    dft, through = sided(table[0]), sided(table[1])
    w = [window_of(wide, at, slot, size) for slot in range(slots)]
    waves = [[(psi[s, m, 0], psi[s, m, 1]) for m in range(modes)] for s in range(slots)]
    fields = [product(waves[s][m], w[s]) for s in range(slots) for m in range(modes)]
    far = both_sides(fields, *dft)
    fields = []
    for s in range(slots):
        own_far = far[s * modes:(s + 1) * modes]
        intensity = sum(re * re + im * im for re, im in own_far)
        live = jnp.where(s < count[0, 0], 2.0, 0.0).astype(F32)
        diff = (intensity - measured[s]) * live
        fields += [(re * diff, -(im * diff)) for re, im in own_far]
    conj = both_sides(fields, *dft)
    fields = [product(conj[s * modes + m], w[s]) for s in range(slots) for m in range(modes)]
    start = both_sides(fields, *through)
    for m in range(modes):
        parts = [product(start[s * modes + m], (window[s, 0], window[s, 1])) for s in range(slots)]
        g_probe[m, 0] = sum(re for re, _ in parts)
        g_probe[m, 1] = -sum(im for _, im in parts)
    for s in range(slots):
        for layer, (grads, by) in enumerate((
            (start, [(probe[m, 0], probe[m, 1]) for m in range(modes)]),
            (conj, waves[s]),
        )):
            parts = [product(grads[s * modes + m], by[m]) for m in range(modes)]
            g_windows[layer, s, 0] = sum(re for re, _ in parts)
            g_windows[layer, s, 1] = -sum(im for _, im in parts)


def object_kernel(at, g_windows, g_upper, g_lower, total):
    layers, slots, _, size, _ = g_windows.shape
    total[...] = jnp.zeros_like(total)
    for s in range(slots):
        for layer in range(layers):
            add_window(total.at[layer], at, s, (g_windows[layer, s, 0], g_windows[layer, s, 1]), size)
    g_upper[...] = total[:, :, :size, :]
    g_lower[...] = total[:, :, size:, :]


VMEM = pl.BlockSpec(memory_space=pltpu.VMEM)
SMEM = pl.BlockSpec(memory_space=pltpu.SMEM)
HBM = pl.BlockSpec(memory_space=pltpu.HBM)


def call(kernel, args, in_specs, outs, scratch, flops):
    args = [
        pltpu.with_memory_space_constraint(a, pltpu.HBM) if spec is HBM else a
        for a, spec in zip(args, in_specs)
    ]
    return pl.pallas_call(
        kernel,
        in_specs=in_specs,
        out_specs=[VMEM] * len(outs),
        out_shape=outs,
        scratch_shapes=scratch,
        compiler_params=pltpu.CompilerParams(vmem_limit_bytes=24 * 1024 * 1024),
        cost_estimate=pl.CostEstimate(flops=flops, bytes_accessed=4 * 1024 * 1024, transcendentals=0),
    )(*args)


def shaped(shape, dtype=F32):
    return jax.ShapeDtypeStruct(shape, dtype)


def on_device(object_slices, probe, measured, offsets, counts):
    layers, _, _, size = object_slices.shape
    slots = offsets.shape[-1]
    modes = probe.shape[0]
    measured = measured.reshape(slots, size, size)
    table = jnp.asarray(tables(size))
    flops = slots * modes * 2 * size * (2 * size) * (6 * size) * 2
    wide = pltpu.VMEM((2, 2 * size, 2 * size), F32)

    right_0 = moved_open(object_slices[0], "tx", -1)
    right_1 = moved_open(object_slices[1], "tx", -1)
    down = moved(object_slices, "ty", -1)
    corner_0 = moved(right_0, "ty", -1)
    corner_1 = moved(right_1, "ty", -1)
    far = (offsets, object_slices, probe, table, measured)
    at, tile, probe_near, table_near, measured_near = call(
        near_kernel, far, [HBM] * len(far), [shaped(a.shape, a.dtype) for a in far],
        [pltpu.SemaphoreType.DMA((len(far),))], 4 * flops,
    )
    psi, window = call(
        first_kernel,
        (at, tile, probe_near, table_near, right_0, down, corner_0),
        [SMEM] + [VMEM] * 6,
        [shaped((slots, modes, 2, size, size)), shaped((slots, 2, size, size))],
        [wide], flops,
    )
    g_probe, g_windows = call(
        second_kernel,
        (at, counts, tile, right_1, down, corner_1, psi, window, probe_near, measured_near, table_near),
        [SMEM] * 2 + [VMEM] * 9,
        [shaped(probe.shape), shaped((layers, slots, 2, size, size))],
        [wide], 3 * flops,
    )

    rows = lax.axis_size("ty")
    part = scattered(g_probe.reshape(-1, size), "ty", 1, 2)
    part, g_windows = lax.optimization_barrier((part, g_windows))
    part = scattered(part, "ty", 2, rows // 2)
    g_upper, g_lower = call(
        object_kernel, (at, g_windows), [SMEM, VMEM],
        [shaped((layers, 2, size, 2 * size))] * 2,
        [pltpu.VMEM((layers, 2, 2 * size, 2 * size), F32)], flops // 4,
    )
    part, g_lower = lax.optimization_barrier((part, g_lower))
    from_above = moved(g_lower, "ty", 1)
    bit = 1
    while bit < lax.axis_size("tx"):
        part = part + swapped(part, "tx", bit)
        bit *= 2
    part, from_above = lax.optimization_barrier((part, from_above))
    g_wide = g_upper + from_above
    g_right, g_own = lax.optimization_barrier((g_wide[..., size:], g_wide[..., :size]))
    from_left_tile = moved(g_right, "tx", 1)
    part, g_right = lax.optimization_barrier((part, g_right))
    part = gathered(part, "ty", 2, rows // 2)
    part = gathered(part, "ty", 1, 2)
    object_grad = g_own + from_left_tile
    return object_grad, part.reshape(probe.shape)


def solution(mesh):
    in_specs = (
        P(None, None, "ty", "tx"),
        P(),
        P("ty", "tx", None, None, None),
        P(None, "ty", "tx", None),
        P("ty", "tx"),
    )
    out_specs = (P(None, None, "ty", "tx"), P())
    return jax.shard_map(
        on_device, mesh=mesh, in_specs=in_specs, out_specs=out_specs, check_vma=False
    )
```

```python
import functools

import jax
import jax.numpy as jnp
import numpy as np
from jax import lax
from jax.experimental import pallas as pl
from jax.experimental.pallas import tpu as pltpu
from jax.sharding import PartitionSpec as P

BF16 = jnp.bfloat16
F32 = jnp.float32


def moved(array, axis, by):
    length = lax.axis_size(axis)
    return lax.ppermute(array, axis, [(i, (i + by) % length) for i in range(length)])


def from_corner(array):
    rows, cols = lax.axis_size("ty"), lax.axis_size("tx")

    def target(a, b):
        if a > 0 and b > 0:
            return a - 1, b - 1
        if a == 0:
            return (rows - 1, b) if b < cols - 1 else (1, b)
        return (a if a > 1 else 0), cols - 1

    pairs = []
    for a in range(rows):
        for b in range(cols):
            down, over = target(a, b)
            pairs.append((a * cols + b, down * cols + over))
    return lax.ppermute(array, ("ty", "tx"), pairs)


def moved_open(array, axis, by):
    length = lax.axis_size(axis)
    return lax.ppermute(array, axis, [(i, i + by) for i in range(length) if 0 <= i + by < length])


def corner_open(array):
    rows, cols = lax.axis_size("ty"), lax.axis_size("tx")
    pairs = [(a * cols + b, (a - 1) * cols + b - 1) for a in range(1, rows) for b in range(1, cols)]
    return lax.ppermute(array, ("ty", "tx"), pairs)


def swapped(array, axis, bit):
    length = lax.axis_size(axis)
    return lax.ppermute(array, axis, [(i, i ^ bit) for i in range(length)])


def picked(array, index):
    return lax.dynamic_index_in_dim(array, index, 0, keepdims=False)


def scattered(part, axis, unit, ways):
    me = (lax.axis_index(axis) // unit) % ways
    blocks = part.reshape(ways, -1, part.shape[-1])
    others = [swapped(picked(blocks, me ^ d), axis, d * unit) for d in range(ways - 1, 0, -1)]
    return functools.reduce(jnp.add, others, picked(blocks, me))


def gathered(part, axis, unit, ways):
    me = (lax.axis_index(axis) // unit) % ways
    out = jnp.zeros((ways,) + part.shape, part.dtype)
    out = lax.dynamic_update_index_in_dim(out, part, me, 0)
    for d in range(ways - 1, 0, -1):
        out = lax.dynamic_update_index_in_dim(out, swapped(part, axis, d * unit), me ^ d, 0)
    return out.reshape(-1, part.shape[-1])


def real_form(table):
    right = np.block([[table.real, table.imag], [-table.imag, table.real]]).astype(np.float32)
    high = right.astype(BF16)
    low = (right - high.astype(np.float32)).astype(BF16)
    return np.stack([high, low])


def tables(size):
    positions = np.arange(size)
    dft = np.exp(-2j * np.pi * (positions[:, None] * positions[None, :] % size) / size) / np.sqrt(size)
    freq = (positions + size // 2) % size - size // 2
    chirp = np.exp(-2j * np.pi * (freq * freq % (4 * size)) / (4 * size))
    through = dft.conj() @ (chirp[:, None] * dft)
    return np.stack([real_form(dft), real_form(through)])


def sided(pair):
    high, low = pair[0], pair[1]
    half = high.shape[0] // 2

    def turned(x):
        return jnp.concatenate(
            [jnp.concatenate([x[:half, :half], x[half:, :half]], axis=1),
             jnp.concatenate([x[:half, half:], x[half:, half:]], axis=1)], axis=0)

    left_high, left_low = turned(high), turned(low)
    return (
        jnp.concatenate([high, high, low], axis=0),
        jnp.concatenate([left_high, left_high, left_low], axis=1),
    )


def halves(x):
    high = x.astype(BF16)
    return high, (x - high.astype(F32)).astype(BF16)


def from_right(x, table):
    high, low = halves(x)
    return jnp.dot(jnp.concatenate([high, low, high], axis=1), table, preferred_element_type=F32)


def from_left(x, table):
    high, low = halves(x)
    return jnp.dot(table, jnp.concatenate([high, low, high], axis=0), preferred_element_type=F32)


def both_sides(fields, right_table, left_table):
    size = fields[0][0].shape[-1]
    done = []
    for first in range(0, len(fields), 2):
        pair = fields[first:first + 2]
        x = jnp.concatenate([jnp.concatenate(field, axis=1) for field in pair], axis=0)
        y = from_right(x, right_table)
        rows = [y[k * size:(k + 1) * size] for k in range(len(pair))]
        y = jnp.concatenate(
            [jnp.concatenate([r[:, :size], r[:, size:]], axis=0) for r in rows], axis=1
        )
        z = from_left(y, left_table)
        for k in range(len(pair)):
            lanes = slice(k * size, (k + 1) * size)
            done.append((z[:size, lanes], z[size:, lanes]))
    return done


def product(a, b):
    return (a[0] * b[0] - a[1] * b[1], a[0] * b[1] + a[1] * b[0])


def fill(wide, own, right, down, corner, size):
    wide[:, :size, :size] = own[...]
    wide[:, :size, size:] = right[...]
    wide[:, size:, :size] = down[...]
    wide[:, size:, size:] = corner[...]


SUBLANES = 8


def window_of(wide, at, slot, size):
    row, col = at[0, 0, 0, slot], at[1, 0, 0, slot]
    shift = lax.rem(row, SUBLANES)
    rows = pl.ds(pl.multiple_of(row - shift, SUBLANES), size + SUBLANES)
    left = lax.rem(2 * size - col, 2 * size)
    up = lax.rem(size + SUBLANES - shift, size + SUBLANES)
    return [
        pltpu.roll(pltpu.roll(wide[c, rows, :], left, axis=1)[:, :size], up, axis=0)[:size]
        for c in range(2)
    ]


def add_window(total, at, slot, grads, size):
    row, col = at[0, 0, 0, slot], at[1, 0, 0, slot]
    shift = lax.rem(row, SUBLANES)
    rows = pl.ds(pl.multiple_of(row - shift, SUBLANES), size + SUBLANES)
    for c in range(2):
        taller = jnp.concatenate([grads[c], jnp.zeros((SUBLANES, size), F32)], axis=0)
        lowered = pltpu.roll(taller, shift, axis=0)
        padded = jnp.concatenate([lowered, jnp.zeros_like(lowered)], axis=1)
        total[c, rows, :] += pltpu.roll(padded, col, axis=1)


def near_kernel(*refs):
    count = (len(refs) - 1) // 2
    copies = [
        pltpu.make_async_copy(refs[i], refs[count + i], refs[-1].at[i]) for i in range(count)
    ]
    for copy in copies:
        copy.start()
    for copy in copies:
        copy.wait()


def first_kernel(at, tile, probe, table, right, down, corner, psi, window, wide):
    size = right.shape[-1]
    slots, modes = psi.shape[:2]
    fill(wide, tile.at[0], right, down.at[0], corner, size)
    fields = []
    for slot in range(slots):
        w = window_of(wide, at, slot, size)
        window[slot, 0], window[slot, 1] = w
        fields += [product((probe[m, 0], probe[m, 1]), w) for m in range(modes)]
    waves = both_sides(fields, *sided(table[1]))
    for i, wave in enumerate(waves):
        psi[i // modes, i % modes, 0], psi[i // modes, i % modes, 1] = wave


def second_kernel(at, count, tile, right, down, corner, psi, window, probe, measured, table,
                  g_probe, g_windows, wide):
    size = right.shape[-1]
    slots, modes = psi.shape[:2]
    fill(wide, tile.at[1], right, down.at[1], corner, size)
    dft, through = sided(table[0]), sided(table[1])
    w = [window_of(wide, at, slot, size) for slot in range(slots)]
    waves = [[(psi[s, m, 0], psi[s, m, 1]) for m in range(modes)] for s in range(slots)]
    fields = [product(waves[s][m], w[s]) for s in range(slots) for m in range(modes)]
    far = both_sides(fields, *dft)
    fields = []
    for s in range(slots):
        own_far = far[s * modes:(s + 1) * modes]
        intensity = sum(re * re + im * im for re, im in own_far)
        live = jnp.where(s < count[0, 0], 2.0, 0.0).astype(F32)
        diff = (intensity - measured[s]) * live
        fields += [(re * diff, -(im * diff)) for re, im in own_far]
    conj = both_sides(fields, *dft)
    fields = [product(conj[s * modes + m], w[s]) for s in range(slots) for m in range(modes)]
    start = both_sides(fields, *through)
    for m in range(modes):
        parts = [product(start[s * modes + m], (window[s, 0], window[s, 1])) for s in range(slots)]
        g_probe[m, 0] = sum(re for re, _ in parts)
        g_probe[m, 1] = -sum(im for _, im in parts)
    for s in range(slots):
        for layer, (grads, by) in enumerate((
            (start, [(probe[m, 0], probe[m, 1]) for m in range(modes)]),
            (conj, waves[s]),
        )):
            parts = [product(grads[s * modes + m], by[m]) for m in range(modes)]
            g_windows[layer, s, 0] = sum(re for re, _ in parts)
            g_windows[layer, s, 1] = -sum(im for _, im in parts)


def object_kernel(at, g_windows, g_upper, g_lower, total):
    layers, slots, _, size, _ = g_windows.shape
    total[...] = jnp.zeros_like(total)
    for s in range(slots):
        for layer in range(layers):
            add_window(total.at[layer], at, s, (g_windows[layer, s, 0], g_windows[layer, s, 1]), size)
    g_upper[...] = total[:, :, :size, :]
    g_lower[...] = total[:, :, size:, :]


VMEM = pl.BlockSpec(memory_space=pltpu.VMEM)
SMEM = pl.BlockSpec(memory_space=pltpu.SMEM)
HBM = pl.BlockSpec(memory_space=pltpu.HBM)


def call(kernel, args, in_specs, outs, scratch, flops):
    args = [
        pltpu.with_memory_space_constraint(a, pltpu.HBM) if spec is HBM else a
        for a, spec in zip(args, in_specs)
    ]
    return pl.pallas_call(
        kernel,
        in_specs=in_specs,
        out_specs=[VMEM] * len(outs),
        out_shape=outs,
        scratch_shapes=scratch,
        compiler_params=pltpu.CompilerParams(vmem_limit_bytes=24 * 1024 * 1024),
        cost_estimate=pl.CostEstimate(flops=flops, bytes_accessed=4 * 1024 * 1024, transcendentals=0),
    )(*args)


def shaped(shape, dtype=F32):
    return jax.ShapeDtypeStruct(shape, dtype)


def on_device(object_slices, probe, measured, offsets, counts):
    layers, _, _, size = object_slices.shape
    slots = offsets.shape[-1]
    modes = probe.shape[0]
    measured = measured.reshape(slots, size, size)
    table = jnp.asarray(tables(size))
    flops = slots * modes * 2 * size * (2 * size) * (6 * size) * 2
    wide = pltpu.VMEM((2, 2 * size, 2 * size), F32)

    right_0 = moved_open(object_slices[0], "tx", -1)
    right_1 = moved_open(object_slices[1], "tx", -1)
    down = moved(object_slices, "ty", -1)
    corner_0 = moved(right_0, "ty", -1)
    corner_1 = moved(right_1, "ty", -1)
    far = (offsets, object_slices, probe, table, measured)
    at, tile, probe_near, table_near, measured_near = call(
        near_kernel, far, [HBM] * len(far), [shaped(a.shape, a.dtype) for a in far],
        [pltpu.SemaphoreType.DMA((len(far),))], 4 * flops,
    )
    psi, window = call(
        first_kernel,
        (at, tile, probe_near, table_near, right_0, down, corner_0),
        [SMEM] + [VMEM] * 6,
        [shaped((slots, modes, 2, size, size)), shaped((slots, 2, size, size))],
        [wide], flops,
    )
    g_probe, g_windows = call(
        second_kernel,
        (at, counts, tile, right_1, down, corner_1, psi, window, probe_near, measured_near, table_near),
        [SMEM] * 2 + [VMEM] * 9,
        [shaped(probe.shape), shaped((layers, slots, 2, size, size))],
        [wide], 3 * flops,
    )

    rows = lax.axis_size("ty")
    part = scattered(g_probe.reshape(-1, size), "ty", 1, 2)
    part, g_windows = lax.optimization_barrier((part, g_windows))
    part = scattered(part, "ty", 2, rows // 2)
    g_upper, g_lower = call(
        object_kernel, (at, g_windows), [SMEM, VMEM],
        [shaped((layers, 2, size, 2 * size))] * 2,
        [pltpu.VMEM((layers, 2, 2 * size, 2 * size), F32)], flops // 4,
    )
    part, g_lower = lax.optimization_barrier((part, g_lower))
    from_above = moved(g_lower, "ty", 1)
    bit = 1
    while bit < lax.axis_size("tx"):
        part = part + swapped(part, "tx", bit)
        bit *= 2
    part, from_above = lax.optimization_barrier((part, from_above))
    g_wide = g_upper + from_above
    g_right, g_own = lax.optimization_barrier((g_wide[..., size:], g_wide[..., :size]))
    from_left_tile = moved(g_right, "tx", 1)
    part, g_right = lax.optimization_barrier((part, g_right))
    part = gathered(part, "ty", 2, rows // 2)
    part = gathered(part, "ty", 1, 2)
    object_grad = g_own + from_left_tile
    return object_grad, part.reshape(probe.shape)


def solution(mesh):
    in_specs = (
        P(None, None, "ty", "tx"),
        P(),
        P("ty", "tx", None, None, None),
        P(None, "ty", "tx", None),
        P("ty", "tx"),
    )
    out_specs = (P(None, None, "ty", "tx"), P())
    return jax.shard_map(
        on_device, mesh=mesh, in_specs=in_specs, out_specs=out_specs, check_vma=False
    )
```
